256 devices in a mesh: dp: 16 (over z, core), head: 16 (over y, x).
Axes of the slice: x: 4, y: 4, z: 8, core: 2. Of those that a mesh axis runs over, the one named last changes fastest.
Arguments:
- states: bfloat16 [8192, 8192], P('dp', 'head'), may hold values from -1000 to 1000
- gain: float32 [8192], P('head'), may hold values from 0.25 to 1.75
- kv_weight: bfloat16 [8192, 2048], P('head'), may hold values from -0.0625 to 0.0625
- kv_bias: float32 [2048], P('head'), may hold values from -3 to 3
- sketch: int32 [2048, 512], P('head'), may hold values from -1 to 1
Outputs:
- basis: float32 [2048, 512], P('head')
- latent: float32 [8192, 512], P('dp', 'head')
The draws below stay inside these ranges and needn't reach their ends.
All inputs are finite; a program needn't handle non-finite values.
Results may differ from the reference program's by a relative error of at most 0.0065.
Values may be sent and summed in bfloat16 or wider, within the bound.
A program may use at most 64 MiB of HBM per device.

```python
import jax
import jax.numpy as jnp
from jax import lax

D = 8192
KVW = 2048
RANK = 512
ITERS = 3
TOK_DEV = 512
TOKENS = 8192
N_DP = 16
N_HEAD = 16


def draw_states(key, part):
    key = jax.random.fold_in(key, 11)
    first, second, third = jax.random.split(key, 3)
    ramp = 3.0 ** (jnp.arange(D, dtype=jnp.float32) / D)
    feature_scale = 10.0 ** (jax.random.uniform(first, (D,), jnp.float32) - 0.5)
    row_scale = 10.0 ** jax.random.uniform(second, (TOKENS, 1), jnp.float32)
    base = jnp.clip(jax.random.normal(third, (TOKENS, D), jnp.float32), -6.0, 6.0)
    return (row_scale * ramp[None, :] * feature_scale[None, :] * base).astype(jnp.bfloat16)


def set_ends(result, own_key, smallest, top_value):
    extent = result.shape
    spot = [jax.random.randint(jax.random.fold_in(own_key, axis), (), 0, extent[axis]) for axis in range(len(extent))]
    result = result.at[tuple(spot)].set(smallest)
    longest = extent.index(max(extent))
    spot[longest] = (spot[longest] + 1) % extent[longest]
    return result.at[tuple(spot)].set(top_value)


def block_scale(stream_key, extent, shards, low, largest):
    loudness = 1.0
    for position, parts in shards:
        heights = jax.random.uniform(jax.random.fold_in(jax.random.fold_in(stream_key, 6), position), (parts,), jnp.float32, low / len(shards), largest / len(shards))
        loudness = loudness * jnp.repeat(jnp.exp(heights), extent[position] // parts).reshape((-1,) + (1,) * (len(extent) - 1 - position))
    return loudness


def noise(own_key, shape, scale, bound, cuts=(), held_as=jnp.bfloat16):
    result = jax.random.normal(own_key, shape, jnp.float32) * scale
    if len(cuts) > 0:
        result = block_scale(own_key, shape, cuts, -0.22, 0.18) * result
    return jnp.clip(result, min=-bound, max=bound).astype(held_as)


def setup_inputs(seed: int = 0) -> dict:
    key_of = jax.random.split(jax.random.key(seed), 6)
    return {
        "states": draw_states(jax.random.fold_in(key_of[5], 71), 0),
        "gain": jnp.clip(1.0 + 0.15 * jax.random.normal(key_of[1], (D,), jnp.float32), 0.25, 1.75),
        "kv_weight": noise(key_of[2], (D, KVW), D ** -0.5, 0.0625, ((0, 16),)),
        "kv_bias": noise(key_of[3], (KVW,), 0.5, 3.0, ((0, 16),), jnp.float32),
        "sketch": set_ends(jax.random.randint(key_of[4], (KVW, RANK), -1, 2), jax.random.fold_in(key_of[4], 1), -1, 1).astype(jnp.int32),
    }


def project(kv_heads, basis):
    groups = kv_heads.shape[0]
    width = kv_heads.shape[2]
    pieces = basis.reshape(groups, width, basis.shape[1])

    def add_group(total, pair):
        block, piece = pair
        part = jnp.dot(block, piece, precision=lax.Precision.HIGHEST)
        return (total + part, None)
    start = jnp.zeros((kv_heads.shape[1], basis.shape[1]), jnp.float32)
    total, unused = lax.scan(add_group, start, (kv_heads, pieces))
    return total

def reference(states, gain, kv_weight, kv_bias, sketch):
    values = states.astype(jnp.float32)
    scale = lax.rsqrt(lax.optimization_barrier(jnp.sum(values * values, axis=1)) / D + 1e-06)
    normed = (values * scale[:, None] * gain[None, :]).astype(jnp.bfloat16)
    weight_full = kv_weight.astype(jnp.float32)
    blocks = normed.reshape(N_DP, TOK_DEV, D)

    def project_block(block):
        out = jnp.dot(block.astype(jnp.float32), weight_full, precision=lax.Precision.HIGHEST)
        return (out + kv_bias[None, :]).astype(jnp.bfloat16)
    keyvals = lax.map(project_block, blocks).reshape(TOKENS, KVW)
    kv_float = keyvals.astype(jnp.float32)
    kv_heads = jnp.transpose(kv_float.reshape(TOKENS, N_HEAD, KVW // N_HEAD), (1, 0, 2))
    basis = sketch.astype(jnp.float32)
    for step in range(ITERS):
        products = project(kv_heads, basis)
        columns = lax.dot_general(kv_float, products, (((0,), (0,)), ((), ())), precision=lax.Precision.HIGHEST)
        gram = lax.dot_general(columns, columns, (((0,), (0,)), ((), ())), precision=lax.Precision.HIGHEST)
        lower = jnp.linalg.cholesky(gram)
        basis = lax.linalg.triangular_solve(lower, columns, left_side=False, lower=True, transpose_a=True)
    latent = project(kv_heads, basis)
    return (basis, latent)
```

```python
import functools

import jax
import jax.numpy as jnp
from jax import lax
from jax.experimental import pallas as pl
from jax.experimental.pallas import tpu as pltpu
from jax.sharding import PartitionSpec as P

D = 8192
F32 = jnp.float32
BF16 = jnp.bfloat16
MESH = pl.DeviceIdType.MESH
VM = pl.BlockSpec(memory_space=pltpu.VMEM)
DMA = pltpu.SemaphoreType.DMA


def position():
    dp, head = lax.axis_index("dp"), lax.axis_index("head")
    return dp, head, dp // 2, dp % 2, head // 4, head % 4


def greet(devices):
    barrier = pltpu.get_barrier_semaphore()
    for device in devices:
        pl.semaphore_signal(barrier, inc=1, device_id=device, device_id_type=MESH)
    pl.semaphore_wait(barrier, len(devices))


class Copies:
    def __init__(self, send_sem, recv_sem):
        self.send_sem, self.recv_sem, self.started = send_sem, recv_sem, []

    def go(self, src, dst, device):
        n = len(self.started)
        copy = pltpu.make_async_remote_copy(
            src_ref=src, dst_ref=dst, send_sem=self.send_sem.at[n],
            recv_sem=self.recv_sem.at[n], device_id=device, device_id_type=MESH,
        )
        copy.start()
        self.started.append(copy)
        return copy

    def finish(self):
        for copy in self.started:
            copy.wait_send()


def params(collective_id=None, mib=48):
    if collective_id is None:
        return pltpu.CompilerParams(vmem_limit_bytes=mib << 20)
    return pltpu.CompilerParams(
        collective_id=collective_id, has_side_effects=True, vmem_limit_bytes=mib << 20
    )


def dot(a, b, dims, precision=None):
    return lax.dot_general(a, b, (dims, ((), ())), precision=precision, preferred_element_type=F32)


NN, NT, TN = ((1,), (0,)), ((1,), (1,)), ((0,), (0,))
HI = lax.Precision.HIGHEST


def split(v):
    high = v.astype(BF16)
    return high, (v - high.astype(F32)).astype(BF16)


def dot3(a, b, dims):
    return dot(a[0], b[0], dims) + (dot(a[0], b[1], dims) + dot(a[1], b[0], dims))


def kv_kernel(st_ref, gain_ref, w_ref, bias_ref, kv_ref, sq_ref, n_ref, own_a, own_b, send_a,
              recv_a, send_b, recv_b, recv2_a, recv2_b, send_sem, recv_sem):
    dp, head, _, _, y, x = position()
    others = [lax.rem(head + k, 16) for k in range(1, 16)]
    xs = [lax.rem(x + k, 4) for k in (1, 2, 3)]
    ys = [lax.rem(y + k, 4) for k in (1, 2, 3)]
    to_x = [(dp, y * 4 + v) for v in xs]
    to_y = [(dp, v * 4 + x) for v in ys]
    copies = Copies(send_sem, recv_sem)

    values = st_ref[...].astype(F32)
    squares = dot(jnp.ones((8, 512), F32), values * values, NT, HI)
    sq_ref[head] = squares
    greet([(dp, v) for v in others])
    arrivals = [copies.go(sq_ref.at[head], sq_ref.at[head], (dp, v)) for v in others]
    for copy in arrivals:
        copy.wait_recv()
    total = sq_ref[0]
    for k in range(1, 16):
        total = total + sq_ref[k]
    scale = lax.rsqrt(total / D + 1e-06)
    column = jnp.transpose(jnp.broadcast_to(scale[0:1], (128, 512)))
    for block in range(4):
        cols = pl.ds(128 * block, 128)
        part = st_ref[:, cols].astype(F32) * column * gain_ref[:, cols]
        n_ref[:, cols] = part.astype(BF16)

    def product(rows, owner):
        cols = pl.ds(pl.multiple_of(owner * 128, 128), 128)
        return dot(n_ref[rows], w_ref[:, cols], NN)

    low, high = pl.ds(0, 256), pl.ds(256, 256)
    first_a, first_b = [], []
    for k in range(3):
        for v in range(4):
            send_a[k, v] = product(low, v * 4 + xs[k]).astype(BF16)
        first_a.append(copies.go(send_a.at[k], recv_a.at[k], to_x[k]))
        for v in range(4):
            send_b[k, v] = product(high, ys[k] * 4 + v).astype(BF16)
        first_b.append(copies.go(send_b.at[k], recv_b.at[k], to_y[k]))
    for v in range(4):
        own_a[v] = product(low, v * 4 + x)
        own_b[v] = product(high, y * 4 + v)
    second_a, second_b = [], []
    for copy in first_a:
        copy.wait_recv()
    for v in range(4):
        own_a[v] += (recv_a[0, v].astype(F32) + recv_a[1, v].astype(F32)) + recv_a[2, v].astype(F32)
    for k in range(3):
        second_a.append(copies.go(own_a.at[ys[k]], recv2_a.at[k], to_y[k]))
    for copy in first_b:
        copy.wait_recv()
    for v in range(4):
        own_b[v] += (recv_b[0, v].astype(F32) + recv_b[1, v].astype(F32)) + recv_b[2, v].astype(F32)
    for k in range(3):
        second_b.append(copies.go(own_b.at[xs[k]], recv2_b.at[k], to_x[k]))
    for copy in second_a:
        copy.wait_recv()
    summed = own_a[y] + (recv2_a[0] + recv2_a[1]) + recv2_a[2]
    kv_ref[y, x, low] = (summed + bias_ref[...]).astype(BF16)
    third_a = [copies.go(kv_ref.at[y, x, low], kv_ref.at[y, x, low], d) for d in to_x]
    for copy in second_b:
        copy.wait_recv()
    summed = own_b[x] + (recv2_b[0] + recv2_b[1]) + recv2_b[2]
    kv_ref[y, x, high] = (summed + bias_ref[...]).astype(BF16)
    third_b = [copies.go(kv_ref.at[y, x, high], kv_ref.at[y, x, high], d) for d in to_y]
    for copy in third_a:
        copy.wait_recv()
    last = [copies.go(kv_ref.at[y, :, low], kv_ref.at[y, :, low], d) for d in to_y]
    for copy in third_b:
        copy.wait_recv()
    last += [copies.go(kv_ref.at[:, x, high], kv_ref.at[:, x, high], d) for d in to_x]
    for copy in last:
        copy.wait_recv()
    copies.finish()


def make_kv(states, gain, weight, bias):
    n = 15 + 6 + 6 + 6 + 6
    return pl.pallas_call(
        kv_kernel,
        out_shape=jax.ShapeDtypeStruct((4, 4, 512, 128), BF16),
        in_specs=[VM] * 4,
        out_specs=VM,
        scratch_shapes=[
            pltpu.VMEM((16, 8, 512), F32),
            pltpu.VMEM((512, 512), BF16),
            pltpu.VMEM((4, 256, 128), F32),
            pltpu.VMEM((4, 256, 128), F32),
            pltpu.VMEM((3, 4, 256, 128), BF16),
            pltpu.VMEM((3, 4, 256, 128), BF16),
            pltpu.VMEM((3, 4, 256, 128), BF16),
            pltpu.VMEM((3, 4, 256, 128), BF16),
            pltpu.VMEM((3, 256, 128), F32),
            pltpu.VMEM((3, 256, 128), F32),
            DMA((n,)),
            DMA((n,)),
        ],
        compiler_params=params(1),
        cost_estimate=pl.CostEstimate(flops=1 << 31, bytes_accessed=100 << 20, transcendentals=0),
    )(states, gain.reshape(1, 512), weight, bias.reshape(1, 128))


def corr_kernel(kv_ref, g_ref, part, recv_half, recv_z, send_sem, recv_sem):
    dp, head, z, c, y, x = position()
    sibling = (dp + 1 - 2 * c, head)
    zs = [lax.rem(z + k, 8) for k in range(1, 8)]
    to_z = [(v * 2 + c, head) for v in zs]
    copies = Copies(send_sem, recv_sem)
    greet([sibling] + to_z)
    for block in range(16):
        part[block // 8, block % 8] = dot(kv_ref[y, x], kv_ref[block // 4, block % 4], TN)
    to_sibling = copies.go(part.at[1 - c], recv_half, sibling)
    to_sibling.wait_recv()
    for block in range(8):
        part[c, block] += recv_half[block]
    first = [copies.go(part.at[c, zs[k]], recv_z.at[k], to_z[k]) for k in range(7)]
    total = part[c, z]
    for k in range(7):
        first[k].wait_recv()
        total = total + recv_z[k]

    def place(owner, half):
        return pl.ds(pl.multiple_of((half * 8 + owner) * 128, 128), 128)

    mine = place(z, c)
    g_ref[:, mine] = total
    second = [copies.go(g_ref.at[:, mine], g_ref.at[:, mine], d) for d in to_z]
    last = [copies.go(g_ref.at[:, mine], g_ref.at[:, mine], sibling)]
    for k in range(7):
        second[k].wait_recv()
        there = place(lax.rem(z + 7 - k, 8), c)
        last.append(copies.go(g_ref.at[:, there], g_ref.at[:, there], sibling))
    for copy in last:
        copy.wait_recv()
    copies.finish()


def make_corr(kv):
    n = 1 + 7 + 7 + 8
    return pl.pallas_call(
        corr_kernel,
        out_shape=jax.ShapeDtypeStruct((128, 2048), F32),
        in_specs=[VM],
        out_specs=VM,
        scratch_shapes=[
            pltpu.VMEM((2, 8, 128, 128), F32),
            pltpu.VMEM((8, 128, 128), F32),
            pltpu.VMEM((7, 128, 128), F32),
            DMA((n,)),
            DMA((n,)),
        ],
        compiler_params=params(2),
    )(kv)


def gather_kernel(x_ref, o_ref, send_sem, recv_sem, own_sem):
    dp, head, _, c, y, x = position()
    rows = x_ref.shape[0]
    quarter = rows // 4
    xs = [lax.rem(x + k, 4) for k in (1, 2, 3)]
    ys = [lax.rem(y + k, 4) for k in (1, 2, 3)]
    to_x = [(dp, y * 4 + v) for v in xs]
    to_y = [(dp, v * 4 + x) for v in ys]
    sibling = (dp + 1 - 2 * c, head)
    copies = Copies(send_sem, recv_sem)
    greet(to_x + to_y + [sibling])
    own = pltpu.make_async_copy(x_ref, o_ref.at[y, x], own_sem)
    own.start()
    a = pl.ds(pl.multiple_of(c * 2 * quarter, quarter), quarter)
    b = pl.ds(pl.multiple_of((c * 2 + 1) * quarter, quarter), quarter)
    first_a = [copies.go(x_ref.at[a], o_ref.at[y, x, a], d) for d in to_x]
    first_b = [copies.go(x_ref.at[b], o_ref.at[y, x, b], d) for d in to_y]
    own.wait()
    for copy in first_a:
        copy.wait_recv()
    second_a = [copies.go(o_ref.at[y, :, a], o_ref.at[y, :, a], d) for d in to_y]
    for copy in first_b:
        copy.wait_recv()
    second_b = [copies.go(o_ref.at[:, x, b], o_ref.at[:, x, b], d) for d in to_x]
    last = []
    for k in range(3):
        vx, vy = lax.rem(x + 3 - k, 4), lax.rem(y + 3 - k, 4)
        last.append(copies.go(o_ref.at[y, vx, a], o_ref.at[y, vx, a], sibling))
        last.append(copies.go(o_ref.at[vy, x, b], o_ref.at[vy, x, b], sibling))
    for k in range(3):
        vx, vy = lax.rem(x + 3 - k, 4), lax.rem(y + 3 - k, 4)
        second_a[k].wait_recv()
        last.append(copies.go(o_ref.at[vy, :, a], o_ref.at[vy, :, a], sibling))
        second_b[k].wait_recv()
        last.append(copies.go(o_ref.at[:, vx, b], o_ref.at[:, vx, b], sibling))
    for copy in last:
        copy.wait_recv()
    copies.finish()


def gather(block, collective_id):
    rows, width = block.shape
    out = pl.pallas_call(
        gather_kernel,
        out_shape=jax.ShapeDtypeStruct((4, 4, rows, width), block.dtype),
        in_specs=[VM],
        out_specs=VM,
        scratch_shapes=[DMA((24,)), DMA((24,)), DMA],
        compiler_params=params(collective_id),
    )(block)
    return out.reshape(16 * rows, width)


def invert_block(a):
    shape = (8, 128)
    rows = [a[8 * g:8 * g + 8] for g in range(16)]
    lane = lax.broadcasted_iota(jnp.int32, shape, 1)
    sub = lax.broadcasted_iota(jnp.int32, shape, 0)
    inverse = [(lane == sub + 8 * g).astype(F32) for g in range(16)]
    for p in range(16):
        spread = [[jnp.broadcast_to(rows[g][:, 8 * p + c:8 * p + c + 1], shape) for g in range(p, 16)]
                  for c in range(8)]
        pivots = None
        for r in range(8):
            pivot = jnp.broadcast_to(spread[r][0][r:r + 1], shape)
            pivots = pivot if pivots is None else jnp.where(sub == r, pivot, pivots)
            recip = 1.0 / pivot
            row = jnp.broadcast_to(rows[p][r:r + 1], shape) * recip
            inverse_row = jnp.broadcast_to(inverse[p][r:r + 1], shape) * recip
            heads = {c: jnp.broadcast_to(spread[c][0][r:r + 1], shape) * recip for c in range(r + 1, 8)}
            for i in range(16 - p):
                if i == 0 and r == 7:
                    continue
                factor = spread[r][i]
                if i == 0:
                    factor = jnp.where(sub > r, factor, 0.0)
                for c in range(r + 1, 8):
                    spread[c][i] = spread[c][i] - factor * heads[c]
                rows[p + i] = rows[p + i] - factor * row
                inverse[p + i] = inverse[p + i] - factor * inverse_row
        inverse[p] = inverse[p] * lax.rsqrt(pivots)
    return jnp.concatenate(inverse, axis=0)


def gram_into(c_ref, a_ref):
    for p in range(4):
        rows = slice(128 * p, 128 * p + 128)
        a_ref[rows, :128 * p + 128] = dot(c_ref[:, rows], c_ref[:, :128 * p + 128], TN, HI)


def invert_factor(a_ref, l_ref, inv_ref):
    inv_ref[...] = jnp.zeros_like(inv_ref)
    for p in range(4):
        here = slice(128 * p, 128 * p + 128)
        block = invert_block(a_ref[here, here])
        if p > 0:
            before = slice(0, 128 * p)
            inv_ref[here, before] = -dot(block, dot(l_ref[here, before], inv_ref[before, before], NN, HI), NN, HI)
        inv_ref[here, here] = block
        if p < 3:
            rest = slice(128 * p + 128, 512)
            panel = dot(a_ref[rest, here], block, NT, HI)
            l_ref[rest, here] = panel
            a_ref[rest, rest] -= dot(panel, panel, NT, HI)


def first_kernel(g_ref, s_ref, o_ref):
    g = split(g_ref[...])
    s = s_ref[...]
    o_ref[...] = dot(g[0], s, NN) + dot(g[1], s, NN)


def first_columns(corr, sketch):
    return pl.pallas_call(
        first_kernel, out_shape=jax.ShapeDtypeStruct((128, 512), F32),
        in_specs=[VM] * 2, out_specs=VM, compiler_params=params(),
    )(corr, sketch)


def step_kernel(c_ref, g_ref, o_ref, a_ref, l_ref, inv_ref, qh_ref, ql_ref):
    gram_into(c_ref, a_ref)
    invert_factor(a_ref, l_ref, inv_ref)
    for p in range(4):
        rows = slice(128 * p, 128 * p + 128)
        upto = slice(0, 128 * p + 128)
        high, low = split(dot3(split(c_ref[:, upto]), split(inv_ref[rows, upto]), NT))
        qh_ref[:, rows] = high
        ql_ref[:, rows] = low
    o_ref[...] = dot3(split(g_ref[...]), (qh_ref[...], ql_ref[...]), NN)


SQUARE = pltpu.VMEM((512, 512), F32)


def step(columns, corr):
    return pl.pallas_call(
        step_kernel, out_shape=jax.ShapeDtypeStruct((128, 512), F32),
        in_specs=[VM] * 2, out_specs=VM,
        scratch_shapes=[SQUARE] * 3 + [pltpu.VMEM((2048, 512), BF16)] * 2,
        compiler_params=params(),
    )(columns, corr)


def last_kernel(c_ref, own_ref, kv_ref, basis_ref, latent_ref, a_ref, l_ref, inv_ref):
    head = lax.axis_index("head")
    gram_into(c_ref, a_ref)
    invert_factor(a_ref, l_ref, inv_ref)
    basis_ref[...] = dot(own_ref[...], inv_ref[...], NT, HI)
    mine = inv_ref[pl.ds(pl.multiple_of(head * 32, 32), 32), :]
    high, low = split(dot(c_ref[...], mine, NT, HI))
    total = jnp.zeros((512, 32), F32)
    for block in range(16):
        rows = slice(128 * block, 128 * block + 128)
        kv = kv_ref[block // 4, block % 4]
        total = total + (dot(kv, high[rows], NN) + dot(kv, low[rows], NN))
    latent_ref[...] = total


def last(columns, own, kv):
    return pl.pallas_call(
        last_kernel,
        out_shape=(jax.ShapeDtypeStruct((128, 512), F32), jax.ShapeDtypeStruct((512, 32), F32)),
        in_specs=[VM] * 3, out_specs=(VM, VM),
        scratch_shapes=[SQUARE] * 3,
        compiler_params=params(),
    )(columns, own, kv)


def local(states, gain, kv_weight, kv_bias, sketch):
    whole_sketch = lax.all_gather(sketch.astype(BF16), "head", axis=0, tiled=True)
    kv = make_kv(states, gain, kv_weight, kv_bias)
    corr = make_corr(kv)
    own = first_columns(corr, whole_sketch)
    columns = gather(own, 3)
    own = step(columns, corr)
    columns = gather(own, 3)
    own = step(columns, corr)
    columns = gather(own, 3)
    return last(columns, own, kv)


def solution(mesh):
    in_specs = (P("dp", "head"), P("head"), P("head", None), P("head"), P("head", None))
    out_specs = (P("head", None), P("dp", "head"))
    return jax.shard_map(local, mesh=mesh, in_specs=in_specs, out_specs=out_specs, check_vma=False)
```

```python
import jax
import jax.numpy as jnp
from jax import lax
from jax.experimental import pallas as pl
from jax.experimental.pallas import tpu as pltpu
from jax.sharding import PartitionSpec as P

D = 8192
F32 = jnp.float32
BF16 = jnp.bfloat16
MESH = pl.DeviceIdType.MESH
VM = pl.BlockSpec(memory_space=pltpu.VMEM)
DMA = pltpu.SemaphoreType.DMA


def position():
    dp, head = lax.axis_index("dp"), lax.axis_index("head")
    return dp, head, dp // 2, dp % 2, head // 4, head % 4


def greet(devices):
    barrier = pltpu.get_barrier_semaphore()
    for device in devices:
        pl.semaphore_signal(barrier, inc=1, device_id=device, device_id_type=MESH)
    pl.semaphore_wait(barrier, len(devices))


class Copies:
    def __init__(self, send_sem, recv_sem):
        self.send_sem, self.recv_sem, self.started = send_sem, recv_sem, []

    def go(self, src, dst, device):
        n = len(self.started)
        copy = pltpu.make_async_remote_copy(
            src_ref=src, dst_ref=dst, send_sem=self.send_sem.at[n],
            recv_sem=self.recv_sem.at[n], device_id=device, device_id_type=MESH,
        )
        copy.start()
        self.started.append(copy)
        return copy

    def finish(self):
        for copy in self.started:
            copy.wait_send()


def params(collective_id=None, mib=48):
    if collective_id is None:
        return pltpu.CompilerParams(vmem_limit_bytes=mib << 20)
    return pltpu.CompilerParams(
        collective_id=collective_id, has_side_effects=True, vmem_limit_bytes=mib << 20
    )


def dot(a, b, dims, precision=None):
    return lax.dot_general(a, b, (dims, ((), ())), precision=precision, preferred_element_type=F32)


NN, NT, TN = ((1,), (0,)), ((1,), (1,)), ((0,), (0,))
HI = lax.Precision.HIGHEST


def split(v):
    high = v.astype(BF16)
    return high, (v - high.astype(F32)).astype(BF16)


def kv_kernel(st_ref, gain_ref, w_ref, bias_ref, sketch_ref, kv_ref, whole_ref, sq_ref, n_ref, own_a, own_b,
              send_a, recv_a, send_b, recv_b, recv2_a, recv2_b, send_sem, recv_sem):
    dp, head, _, c, y, x = position()
    sibling = (dp + 1 - 2 * c, head)
    half = pl.ds(pl.multiple_of(c * 64, 64), 64)
    part_a = pl.ds(pl.multiple_of(c * 64, 32), 32)
    part_b = pl.ds(pl.multiple_of(c * 64 + 32, 32), 32)
    others = [lax.rem(head + k, 16) for k in range(1, 16)]
    xs = [lax.rem(x + k, 4) for k in (1, 2, 3)]
    ys = [lax.rem(y + k, 4) for k in (1, 2, 3)]
    to_x = [(dp, y * 4 + v) for v in xs]
    to_y = [(dp, v * 4 + x) for v in ys]
    copies = Copies(send_sem, recv_sem)

    values = st_ref[...].astype(F32)
    squares = dot(jnp.ones((8, 512), F32), values * values, NT, HI)
    sq_ref[head] = squares
    whole_ref[y, x, half] = sketch_ref[half].astype(BF16)
    greet([(dp, v) for v in others] + [sibling])
    arrivals = [copies.go(sq_ref.at[head], sq_ref.at[head], (dp, v)) for v in others]
    spread_a = [copies.go(whole_ref.at[y, x, part_a], whole_ref.at[y, x, part_a], d) for d in to_x]
    spread_b = [copies.go(whole_ref.at[y, x, part_b], whole_ref.at[y, x, part_b], d) for d in to_y]
    for copy in arrivals:
        copy.wait_recv()
    total = sq_ref[0]
    for k in range(1, 16):
        total = total + sq_ref[k]
    scale = lax.rsqrt(total / D + 1e-06)
    column = jnp.transpose(jnp.broadcast_to(scale[0:1], (128, 512)))
    for block in range(4):
        cols = pl.ds(128 * block, 128)
        part = st_ref[:, cols].astype(F32) * column * gain_ref[:, cols]
        n_ref[:, cols] = part.astype(BF16)

    def product(rows, owner):
        cols = pl.ds(pl.multiple_of(owner * 128, 128), 128)
        return dot(n_ref[rows], w_ref[:, cols], NN)

    for copy in spread_a + spread_b:
        copy.wait_recv()
    spread = [copies.go(whole_ref.at[y, :, part_a], whole_ref.at[y, :, part_a], d) for d in to_y]
    spread += [copies.go(whole_ref.at[:, x, part_b], whole_ref.at[:, x, part_b], d) for d in to_x]
    low, high = pl.ds(0, 256), pl.ds(256, 256)
    first_a, first_b = [], []
    for k in range(3):
        for v in range(4):
            send_a[k, v] = product(low, v * 4 + xs[k]).astype(BF16)
        first_a.append(copies.go(send_a.at[k], recv_a.at[k], to_x[k]))
        for v in range(4):
            send_b[k, v] = product(high, ys[k] * 4 + v).astype(BF16)
        first_b.append(copies.go(send_b.at[k], recv_b.at[k], to_y[k]))
    for v in range(4):
        own_a[v] = product(low, v * 4 + x)
        own_b[v] = product(high, y * 4 + v)
    second_a, second_b = [], []
    for copy in first_a:
        copy.wait_recv()
    for v in range(4):
        own_a[v] += (recv_a[0, v].astype(F32) + recv_a[1, v].astype(F32)) + recv_a[2, v].astype(F32)
    for k in range(3):
        second_a.append(copies.go(own_a.at[ys[k]], recv2_a.at[k], to_y[k]))
    for copy in first_b:
        copy.wait_recv()
    for v in range(4):
        own_b[v] += (recv_b[0, v].astype(F32) + recv_b[1, v].astype(F32)) + recv_b[2, v].astype(F32)
    for k in range(3):
        second_b.append(copies.go(own_b.at[xs[k]], recv2_b.at[k], to_x[k]))
    for copy in spread:
        copy.wait_recv()
    spread = [copies.go(whole_ref.at[:, :, half], whole_ref.at[:, :, half], sibling)]
    for copy in second_a:
        copy.wait_recv()
    summed = own_a[y] + (recv2_a[0] + recv2_a[1]) + recv2_a[2]
    kv_ref[y, x, low] = (summed + bias_ref[...]).astype(BF16)
    third_a = [copies.go(kv_ref.at[y, x, low], kv_ref.at[y, x, low], d) for d in to_x]
    for copy in second_b:
        copy.wait_recv()
    summed = own_b[x] + (recv2_b[0] + recv2_b[1]) + recv2_b[2]
    kv_ref[y, x, high] = (summed + bias_ref[...]).astype(BF16)
    third_b = [copies.go(kv_ref.at[y, x, high], kv_ref.at[y, x, high], d) for d in to_y]
    for copy in third_a:
        copy.wait_recv()
    last = [copies.go(kv_ref.at[y, :, low], kv_ref.at[y, :, low], d) for d in to_y]
    for copy in third_b:
        copy.wait_recv()
    last += [copies.go(kv_ref.at[:, x, high], kv_ref.at[:, x, high], d) for d in to_x]
    for copy in last + spread:
        copy.wait_recv()
    copies.finish()


def make_kv(states, gain, weight, bias, sketch):
    n = 15 + 6 + 6 + 6 + 6 + 13
    return pl.pallas_call(
        kv_kernel,
        out_shape=(
            jax.ShapeDtypeStruct((4, 4, 512, 128), BF16),
            jax.ShapeDtypeStruct((4, 4, 128, 512), BF16),
        ),
        in_specs=[VM] * 5,
        out_specs=(VM, VM),
        scratch_shapes=[
            pltpu.VMEM((16, 8, 512), F32),
            pltpu.VMEM((512, 512), BF16),
            pltpu.VMEM((4, 256, 128), F32),
            pltpu.VMEM((4, 256, 128), F32),
            pltpu.VMEM((3, 4, 256, 128), BF16),
            pltpu.VMEM((3, 4, 256, 128), BF16),
            pltpu.VMEM((3, 4, 256, 128), BF16),
            pltpu.VMEM((3, 4, 256, 128), BF16),
            pltpu.VMEM((3, 256, 128), F32),
            pltpu.VMEM((3, 256, 128), F32),
            DMA((n,)),
            DMA((n,)),
        ],
        compiler_params=params(1),
    )(states, gain.reshape(1, 512), weight, bias.reshape(1, 128), sketch)


def corr_kernel(kv_ref, g_ref, part, recv_half, recv_z, send_sem, recv_sem):
    dp, head, z, c, y, x = position()
    sibling = (dp + 1 - 2 * c, head)
    zs = [lax.rem(z + k, 8) for k in range(1, 8)]
    to_z = [(v * 2 + c, head) for v in zs]
    copies = Copies(send_sem, recv_sem)
    greet([sibling] + to_z)
    for block in range(16):
        cols = pl.ds(block % 2 * 128, 128)
        value = dot(kv_ref[y, x], kv_ref[block // 4, block % 4], TN)
        part[0, block // 2, :, cols] = value[:64]
        part[1, block // 2, :, cols] = value[64:]
    to_sibling = copies.go(part.at[1 - c], recv_half, sibling)
    to_sibling.wait_recv()
    for block in range(8):
        part[c, block] += recv_half[block]
    first = [copies.go(part.at[c, zs[k]], recv_z.at[k], to_z[k]) for k in range(7)]
    total = part[c, z]
    for k in range(7):
        first[k].wait_recv()
        total = total + recv_z[k]
    mine = pl.ds(pl.multiple_of(z * 256, 256), 256)
    g_ref[:, mine] = total
    second = [copies.go(g_ref.at[:, mine], g_ref.at[:, mine], d) for d in to_z]
    for copy in second:
        copy.wait_recv()
    copies.finish()


def make_corr(kv):
    n = 1 + 7 + 7
    return pl.pallas_call(
        corr_kernel,
        out_shape=jax.ShapeDtypeStruct((64, 2048), F32),
        in_specs=[VM],
        out_specs=VM,
        scratch_shapes=[
            pltpu.VMEM((2, 8, 64, 256), F32),
            pltpu.VMEM((8, 64, 256), F32),
            pltpu.VMEM((7, 64, 256), F32),
            DMA((n,)),
            DMA((n,)),
        ],
        compiler_params=params(2),
    )(kv)


def invert_block(a):
    shape = (8, 128)
    rows = [a[8 * g:8 * g + 8] for g in range(16)]
    lane = lax.broadcasted_iota(jnp.int32, shape, 1)
    sub = lax.broadcasted_iota(jnp.int32, shape, 0)
    inverse = [(lane == sub + 8 * g).astype(F32) for g in range(16)]
    for p in range(16):
        spread = [[jnp.broadcast_to(rows[g][:, 8 * p + c:8 * p + c + 1], shape) for g in range(p, 16)]
                  for c in range(8)]
        pivots = None
        for r in range(8):
            pivot = jnp.broadcast_to(spread[r][0][r:r + 1], shape)
            pivots = pivot if pivots is None else jnp.where(sub == r, pivot, pivots)
            recip = 1.0 / pivot
            row = jnp.broadcast_to(rows[p][r:r + 1], shape) * recip
            inverse_row = jnp.broadcast_to(inverse[p][r:r + 1], shape) * recip
            heads = {c: jnp.broadcast_to(spread[c][0][r:r + 1], shape) * recip for c in range(r + 1, 8)}
            for i in range(16 - p):
                if i == 0 and r == 7:
                    continue
                factor = spread[r][i]
                if i == 0:
                    factor = jnp.where(sub > r, factor, 0.0)
                for c in range(r + 1, 8):
                    spread[c][i] = spread[c][i] - factor * heads[c]
                rows[p + i] = rows[p + i] - factor * row
                inverse[p + i] = inverse[p + i] - factor * inverse_row
        inverse[p] = inverse[p] * lax.rsqrt(pivots)
    return jnp.concatenate(inverse, axis=0)


def order(t):
    r = t % 4
    return t + (r // 3) * (1 - t // 11) - (1 - (r + 3) // 4) * ((t + 11) // 12)


def beside(v):
    return jnp.concatenate(split(v), axis=1)


def halves(v):
    return v[:, :128] + v[:, 128:]


def quarters(v):
    rows = v.shape[0] // 2
    return halves(v[:rows]) + halves(v[rows:])


def iterate_kernel(g_ref, s_ref, kv_ref, basis_ref, latent_ref, cols_ref, q_ref, pair_ref, send_sem, recv_sem):
    dp, head, _, c, y, x = position()
    xs = [lax.rem(x + k, 4) for k in (1, 2, 3)]
    ys = [lax.rem(y + k, 4) for k in (1, 2, 3)]
    to_x = [(dp, y * 4 + v) for v in xs]
    to_y = [(dp, v * 4 + x) for v in ys]
    sibling = (dp + 1 - 2 * c, head)
    half = pl.ds(pl.multiple_of(c * 64, 64), 64)
    part_a = pl.ds(pl.multiple_of(c * 64, 32), 32)
    part_b = pl.ds(pl.multiple_of(c * 64 + 32, 32), 32)
    greet(to_x + to_y + [sibling])

    def copy(kp, n, where, device):
        here = cols_ref.at[(kp,) + where]
        return pltpu.make_async_remote_copy(
            src_ref=here, dst_ref=here, send_sem=send_sem.at[kp, n], recv_sem=recv_sem.at[kp, n],
            device_id=device, device_id_type=MESH,
        )

    every = slice(None)

    def first(kp):
        return [copy(kp, n, (y, x, part_a), to_x[n]) for n in range(3)] + [
            copy(kp, 3 + n, (y, x, part_b), to_y[n]) for n in range(3)]

    def second(kp):
        return [copy(kp, 6 + n, (y, every, part_a), to_y[n]) for n in range(3)] + [
            copy(kp, 9 + n, (every, x, part_b), to_x[n]) for n in range(3)]

    def third(kp):
        return [copy(kp, 12, (every, every, half), sibling)]

    def go(some):
        for one in some:
            one.start()

    def arrive(some):
        for one in some:
            one.wait_recv()

    def leave(some):
        for one in some:
            one.wait_send()

    pair_ref[:64], pair_ref[64:] = split(g_ref[...])
    for p in range(4):
        s = s_ref[:, :, :, 128 * p:128 * p + 128].reshape(2048, 128)
        new = dot(pair_ref[...], s, NN)
        cols_ref[p, y, x, half] = beside(new[:64] + new[64:])
        go(first(p))
    for p in range(4):
        arrive(first(p))
        go(second(p))
    arrive(second(0))
    go(third(0))

    def task(t, carry):
        kp = order(t)
        k, p = kp // 4, kp % 4
        arrive(third(kp))
        leave(first(kp) + second(kp) + third(kp))

        def subtract(q, carry):
            other = q_ref[k * 4 + q]
            now = cols_ref[kp].reshape(2048, 256)
            factor = beside(quarters(dot(other, now, TN)))
            weights = jnp.concatenate([factor, factor], axis=0)
            for r in range(4):
                rows = pl.ds(512 * r, 512)
                taken = halves(dot(q_ref[k * 4 + q, rows], weights, NN))
                old = cols_ref[kp, r].reshape(512, 256).astype(F32)
                cols_ref[kp, r] = beside(halves(old) - taken).reshape(4, 128, 256)
            return carry

        lax.fori_loop(0, p, subtract, 0)

        @pl.when((t >= 2) & (order(t - 2 + 2 * (1 - (t + 10) // 12)) < 8))
        def _():
            due = order(t - 2) + 4
            arrive(second(due))
            go(third(due))

        @pl.when(t < 3)
        def _():
            arrive(second(t + 1))
            go(third(t + 1))

        now = cols_ref[kp].reshape(2048, 256)
        block = invert_block(quarters(dot(now, now, TN)))

        @pl.when((t >= 1) & (order(t - 1 + (1 - (t + 11) // 12)) < 8))
        def _():
            due = order(t - 1) + 4
            arrive(first(due))
            go(second(due))

        high, low = split(block)
        weights = jnp.concatenate(
            [jnp.concatenate([high, high], axis=1), jnp.concatenate([low, low], axis=1)], axis=0)
        for r in range(4):
            rows = pl.ds(512 * r, 512)
            q_ref[kp, rows] = beside(halves(dot(cols_ref[kp, r].reshape(512, 256), weights, NT)))

        @pl.when(k < 2)
        def _():
            cols_ref[kp + 4, y, x, half] = beside(quarters(dot(pair_ref[...], q_ref[kp], NN)))
            go(first(kp + 4))

        @pl.when(k == 2)
        def _():
            rows = pl.ds(pl.multiple_of(head * 128, 128), 128)
            basis_ref[:, pl.ds(pl.multiple_of(p * 128, 128), 128)] = halves(q_ref[kp, rows].astype(F32))

        return carry

    lax.fori_loop(0, 12, task, 0)
    total = jnp.zeros((512, 256), F32)
    for block in range(16):
        kv = kv_ref[block // 4, block % 4]
        total = total + dot(kv, q_ref[8 + head // 4, 128 * block:128 * block + 128], NN)
    total = halves(total)
    for n in range(4):
        @pl.when(head % 4 == n)
        def _():
            latent_ref[...] = total[:, 32 * n:32 * n + 32]


def iterate(corr, sketch, kv):
    return pl.pallas_call(
        iterate_kernel,
        out_shape=(jax.ShapeDtypeStruct((128, 512), F32), jax.ShapeDtypeStruct((512, 32), F32)),
        in_specs=[VM] * 3, out_specs=(VM, VM),
        scratch_shapes=[
            pltpu.VMEM((12, 4, 4, 128, 256), BF16),
            pltpu.VMEM((12, 2048, 256), BF16),
            pltpu.VMEM((128, 2048), BF16),
            DMA((12, 13)),
            DMA((12, 13)),
        ],
        compiler_params=params(3),
    )(corr, sketch, kv)


def local(states, gain, kv_weight, kv_bias, sketch):
    kv, whole_sketch = make_kv(states, gain, kv_weight, kv_bias, sketch)
    return iterate(make_corr(kv), whole_sketch, kv)


def solution(mesh):
    in_specs = (P("dp", "head"), P("head"), P("head", None), P("head"), P("head", None))
    out_specs = (P("head", None), P("dp", "head"))
    return jax.shard_map(local, mesh=mesh, in_specs=in_specs, out_specs=out_specs, check_vma=False)
```

```python
import jax
import jax.numpy as jnp
from jax import lax
from jax.experimental import pallas as pl
from jax.experimental.pallas import tpu as pltpu
from jax.sharding import PartitionSpec as P

D = 8192
F32 = jnp.float32
BF16 = jnp.bfloat16
MESH = pl.DeviceIdType.MESH
VM = pl.BlockSpec(memory_space=pltpu.VMEM)
DMA = pltpu.SemaphoreType.DMA


def position():
    dp, head = lax.axis_index("dp"), lax.axis_index("head")
    return dp, head, dp // 2, dp % 2, head // 4, head % 4


def greet(devices):
    barrier = pltpu.get_barrier_semaphore()
    for device in devices:
        pl.semaphore_signal(barrier, inc=1, device_id=device, device_id_type=MESH)
    pl.semaphore_wait(barrier, len(devices))


class Copies:
    def __init__(self, send_sem, recv_sem):
        self.send_sem, self.recv_sem, self.started = send_sem, recv_sem, []

    def go(self, src, dst, device):
        n = len(self.started)
        copy = pltpu.make_async_remote_copy(
            src_ref=src, dst_ref=dst, send_sem=self.send_sem.at[n],
            recv_sem=self.recv_sem.at[n], device_id=device, device_id_type=MESH,
        )
        copy.start()
        self.started.append(copy)
        return copy

    def finish(self):
        for copy in self.started:
            copy.wait_send()


def dot(a, b, dims, precision=None):
    return lax.dot_general(a, b, (dims, ((), ())), precision=precision, preferred_element_type=F32)


NN, NT, TN = ((1,), (0,)), ((1,), (1,)), ((0,), (0,))
HI = lax.Precision.HIGHEST


def split(v):
    high = v.astype(BF16)
    return high, (v - high.astype(F32)).astype(BF16)


def make_kv(place, copies, st_ref, gain_ref, w_any, bias_ref, kv_ref, w_ref, sq_ref, n_ref, part_ref, own_ref,
            recv_ref, recv2_ref, w_sem, meet):
    dp, head, _, _, y, x = place
    load = pltpu.make_async_copy(w_any, w_ref, w_sem)
    load.start()
    others = [lax.rem(head + k, 16) for k in range(1, 16)]
    xs = [lax.rem(x + k, 4) for k in (2, 1, 3)]
    ys = [lax.rem(y + k, 4) for k in (2, 1, 3)]
    to_x = [(dp, y * 4 + v) for v in xs]
    to_y = [(dp, v * 4 + x) for v in ys]

    values = st_ref[...].astype(F32)
    sq_ref[head] = dot(jnp.ones((8, 512), F32), values * values, NT, HI)
    meet()
    arrivals = [copies.go(sq_ref.at[head, 0:1], sq_ref.at[head, 0:1], (dp, v)) for v in others]
    for copy in arrivals:
        copy.wait_recv()
    total = sq_ref[0, 0:1]
    for k in range(1, 16):
        total = total + sq_ref[k, 0:1]
    scale = lax.rsqrt(total / D + 1e-06)
    column = jnp.transpose(jnp.broadcast_to(scale, (128, 512)))
    for block in range(4):
        cols = pl.ds(128 * block, 128)
        part = st_ref[:, cols].astype(F32) * column * gain_ref[:, cols]
        n_ref[:, cols] = part.astype(BF16)
    load.wait()

    def product(rows, owner):
        cols = pl.ds(pl.multiple_of(owner * 128, 128), 128)
        return dot(n_ref[rows], w_ref[:, cols], NN)

    chunks = [pl.ds(128 * n, 128) for n in range(4)]
    first = [[], [], [], []]
    for k in range(3):
        for v in range(4):
            part_ref[v, xs[k]] = product(pl.ds(0, 512), v * 4 + xs[k]).astype(BF16)
        for n in range(2):
            first[n].append(copies.go(part_ref.at[:, xs[k], chunks[n]], recv_ref.at[n, k], to_x[k]))
    for v in range(4):
        whole = product(pl.ds(0, 512), v * 4 + x)
        part_ref[v, x] = whole.astype(BF16)
        own_ref[0, v] = whole[:128]
        own_ref[1, v] = whole[128:256]
    for n in range(2, 4):
        for k in range(3):
            first[n].append(copies.go(part_ref.at[ys[k], :, chunks[n]], recv_ref.at[n, k], to_y[k]))
    for v in range(4):
        own = product(pl.ds(256, 256), y * 4 + v)
        own_ref[2, v] = own[:128]
        own_ref[3, v] = own[128:]
    sequence = (0, 2, 1, 3)
    second = [None] * 4
    for n in sequence:
        for copy in first[n]:
            copy.wait_recv()
        for v in range(4):
            own_ref[n, v] += (recv_ref[n, 0, v].astype(F32) + recv_ref[n, 1, v].astype(F32)) + recv_ref[
                n, 2, v].astype(F32)
        far, to = (ys, to_y) if n < 2 else (xs, to_x)
        second[n] = [copies.go(own_ref.at[n, far[k]], recv2_ref.at[n, k], to[k]) for k in range(3)]
    third = [None] * 4
    for n in sequence:
        for copy in second[n]:
            copy.wait_recv()
        summed = own_ref[n, y if n < 2 else x] + (recv2_ref[n, 0] + recv2_ref[n, 1]) + recv2_ref[n, 2]
        kv_ref[y, x, chunks[n]] = (summed + bias_ref[...]).astype(BF16)
        block = kv_ref.at[y, x, chunks[n]]
        third[n] = [copies.go(block, block, d) for d in (to_x if n < 2 else to_y)]
    fourth = []
    for n in sequence:
        for copy in third[n]:
            copy.wait_recv()
        line = kv_ref.at[y, :, chunks[n]] if n < 2 else kv_ref.at[:, x, chunks[n]]
        fourth += [copies.go(line, line, d) for d in (to_y if n < 2 else to_x)]
    for copy in fourth:
        copy.wait_recv()


def make_corr(place, copies, kv_ref, sketch_ref, whole_ref, part, recv_half, recv_z, g_ref):
    dp, head, z, c, y, x = place
    sibling = (dp + 1 - 2 * c, head)
    zs = [lax.rem(z + k, 8) for k in (4, 3, 5, 2, 6, 1, 7)]
    to_z = [(v * 2 + c, head) for v in zs]
    to_x = [(dp, y * 4 + lax.rem(x + k, 4)) for k in (1, 2, 3)]
    to_y = [(dp, lax.rem(y + k, 4) * 4 + x) for k in (1, 2, 3)]
    half = pl.ds(pl.multiple_of(c * 64, 64), 64)
    part_a = pl.ds(pl.multiple_of(c * 64, 32), 32)
    part_b = pl.ds(pl.multiple_of(c * 64 + 32, 32), 32)
    whole_ref[y, x, half] = sketch_ref[half].astype(BF16)
    spread_a = [copies.go(whole_ref.at[y, x, part_a], whole_ref.at[y, x, part_a], d) for d in to_x]
    spread_b = [copies.go(whole_ref.at[y, x, part_b], whole_ref.at[y, x, part_b], d) for d in to_y]
    mine = kv_ref[y, x]
    for owner in range(8):
        pair = jnp.concatenate([kv_ref[owner // 2, owner % 2 * 2], kv_ref[owner // 2, owner % 2 * 2 + 1]], axis=1)
        value = dot(mine, pair, TN)
        part[0, owner] = value[:64]
        part[1, owner] = value[64:]
    swaps = [copies.go(part.at[1 - c, v], recv_half.at[v], sibling) for v in zs + [z]]
    for copy in spread_a + spread_b:
        copy.wait_recv()
    spread = [copies.go(whole_ref.at[y, :, part_a], whole_ref.at[y, :, part_a], d) for d in to_y]
    spread += [copies.go(whole_ref.at[:, x, part_b], whole_ref.at[:, x, part_b], d) for d in to_x]
    first = []
    for k in range(7):
        swaps[k].wait_recv()
        part[c, zs[k]] += recv_half[zs[k]]
        first.append(copies.go(part.at[c, zs[k]], recv_z.at[k], to_z[k]))
    swaps[7].wait_recv()
    total = part[c, z] + recv_half[z]
    for k in range(7):
        first[k].wait_recv()
        total = total + recv_z[k]
    cols = pl.ds(pl.multiple_of(z * 256, 256), 256)
    g_ref[:, cols] = total
    second = [copies.go(g_ref.at[:, cols], g_ref.at[:, cols], d) for d in to_z]
    for copy in spread:
        copy.wait_recv()
    last = copies.go(whole_ref.at[:, :, half], whole_ref.at[:, :, half], sibling)
    for copy in second:
        copy.wait_recv()
    last.wait_recv()


def invert_block(a):
    shape = (8, 128)
    rows = [a[8 * g:8 * g + 8] for g in range(16)]
    lane = lax.broadcasted_iota(jnp.int32, shape, 1)
    sub = lax.broadcasted_iota(jnp.int32, shape, 0)
    inverse = [(lane == sub + 8 * g).astype(F32) for g in range(16)]
    for p in range(16):
        spread = [[jnp.broadcast_to(rows[g][:, 8 * p + c:8 * p + c + 1], shape) for g in range(p, 16)]
                  for c in range(8)]
        pivots = None
        for r in range(8):
            pivot = jnp.broadcast_to(spread[r][0][r:r + 1], shape)
            pivots = pivot if pivots is None else jnp.where(sub == r, pivot, pivots)
            recip = 1.0 / pivot
            row = jnp.broadcast_to(rows[p][r:r + 1], shape) * recip
            inverse_row = jnp.broadcast_to(inverse[p][r:r + 1], shape) * recip
            heads = {c: jnp.broadcast_to(spread[c][0][r:r + 1], shape) * recip for c in range(r + 1, 8)}
            for i in range(16 - p):
                if i == 0 and r == 7:
                    continue
                factor = spread[r][i]
                if i == 0:
                    factor = jnp.where(sub > r, factor, 0.0)
                for c in range(r + 1, 8):
                    spread[c][i] = spread[c][i] - factor * heads[c]
                rows[p + i] = rows[p + i] - factor * row
                inverse[p + i] = inverse[p + i] - factor * inverse_row
        inverse[p] = inverse[p] * lax.rsqrt(pivots)
    return jnp.concatenate(inverse, axis=0)


def order(t):
    r = t % 4
    return t + (r // 3) * (1 - t // 11) - (1 - (r + 3) // 4) * ((t + 11) // 12)


def beside(v):
    return jnp.concatenate(split(v), axis=1)


def halves(v):
    return v[:, :128] + v[:, 128:]


def quarters(v):
    rows = v.shape[0] // 2
    return halves(v[:rows]) + halves(v[rows:])


def iterate(place, g_ref, s_ref, kv_ref, basis_ref, latent_ref, cols_ref, q_ref, pair_ref, send_sem, recv_sem):
    dp, head, _, c, y, x = place
    xs = [lax.rem(x + k, 4) for k in (1, 2, 3)]
    ys = [lax.rem(y + k, 4) for k in (1, 2, 3)]
    to_x = [(dp, y * 4 + v) for v in xs]
    to_y = [(dp, v * 4 + x) for v in ys]
    sibling = (dp + 1 - 2 * c, head)
    half = pl.ds(pl.multiple_of(c * 64, 64), 64)
    part_a = pl.ds(pl.multiple_of(c * 64, 32), 32)
    part_b = pl.ds(pl.multiple_of(c * 64 + 32, 32), 32)

    def copy(kp, n, where, device):
        here = cols_ref.at[(kp,) + where]
        return pltpu.make_async_remote_copy(
            src_ref=here, dst_ref=here, send_sem=send_sem.at[kp, n], recv_sem=recv_sem.at[kp, n],
            device_id=device, device_id_type=MESH,
        )

    every = slice(None)

    def first(kp):
        return [copy(kp, n, (y, x, part_a), to_x[n]) for n in range(3)] + [
            copy(kp, 3 + n, (y, x, part_b), to_y[n]) for n in range(3)]

    def second(kp):
        return [copy(kp, 6 + n, (y, every, part_a), to_y[n]) for n in range(3)] + [
            copy(kp, 9 + n, (every, x, part_b), to_x[n]) for n in range(3)]

    def third(kp):
        return [copy(kp, 12, (every, every, half), sibling)]

    def go(some):
        for one in some:
            one.start()

    def arrive(some):
        for one in some:
            one.wait_recv()

    def leave(some):
        for one in some:
            one.wait_send()

    pair_ref[:64], pair_ref[64:] = split(g_ref[...])
    for p in range(4):
        s = s_ref[:, :, :, 128 * p:128 * p + 128].reshape(2048, 128)
        new = dot(pair_ref[...], s, NN)
        cols_ref[p, y, x, half] = beside(new[:64] + new[64:])
        go(first(p))
    for p in range(4):
        arrive(first(p))
        go(second(p))
    arrive(second(0))
    go(third(0))

    def task(t, carry):
        kp = order(t)
        k, p = kp // 4, kp % 4
        arrive(third(kp))
        leave(first(kp) + second(kp) + third(kp))

        for n in range(1, 4):
            @pl.when(p == n)
            def _():
                now = cols_ref[kp].reshape(2048, 256)
                factors = [beside(quarters(dot(q_ref[k * 4 + q], now, TN))) for q in range(n)]
                weights = [jnp.concatenate([factor, factor], axis=0) for factor in factors]
                taken = dot(q_ref[k * 4], weights[0], NN)
                for q in range(1, n):
                    taken = taken + dot(q_ref[k * 4 + q], weights[q], NN)
                cols_ref[kp] = beside(halves(now.astype(F32)) - halves(taken)).reshape(4, 4, 128, 256)

        @pl.when((t >= 2) & (order(t - 2 + 2 * (1 - (t + 10) // 12)) < 8))
        def _():
            due = order(t - 2) + 4
            arrive(second(due))
            go(third(due))

        @pl.when(t < 3)
        def _():
            arrive(second(t + 1))
            go(third(t + 1))

        now = cols_ref[kp].reshape(2048, 256)
        block = invert_block(quarters(dot(now, now, TN)))

        @pl.when((t >= 1) & (order(t - 1 + (1 - (t + 11) // 12)) < 8))
        def _():
            due = order(t - 1) + 4
            arrive(first(due))
            go(second(due))

        high, low = split(block)
        weights = jnp.concatenate(
            [jnp.concatenate([high, high], axis=1), jnp.concatenate([low, low], axis=1)], axis=0)
        for r in range(4):
            rows = pl.ds(512 * r, 512)
            q_ref[kp, rows] = beside(halves(dot(cols_ref[kp, r].reshape(512, 256), weights, NT)))

        @pl.when(k < 2)
        def _():
            cols_ref[kp + 4, y, x, half] = beside(quarters(dot(pair_ref[...], q_ref[kp], NN)))
            go(first(kp + 4))

        @pl.when(k == 2)
        def _():
            rows = pl.ds(pl.multiple_of(head * 128, 128), 128)
            basis_ref[:, pl.ds(pl.multiple_of(p * 128, 128), 128)] = halves(q_ref[kp, rows].astype(F32))

        return carry

    lax.fori_loop(0, 12, task, 0)
    total = jnp.zeros((512, 256), F32)
    for block in range(16):
        kv = kv_ref[block // 4, block % 4]
        total = total + dot(kv, q_ref[8 + head // 4, 128 * block:128 * block + 128], NN)
    total = halves(total)
    for n in range(4):
        @pl.when(head % 4 == n)
        def _():
            latent_ref[...] = total[:, 32 * n:32 * n + 32]


def kernel(st_ref, gain_ref, w_any, bias_ref, sketch_ref, basis_ref, latent_ref, kv_ref, w_ref, sq_ref, n_ref,
           part_ref, own_ref, recv_ref, recv2_ref, whole_ref, gpart_ref, half_ref, z_ref, g_ref, cols_ref, q_ref,
           pair_ref, w_sem, send_sem, recv_sem, panel_send, panel_recv):
    place = position()
    dp, head, z, c, _, _ = place
    copies = Copies(send_sem, recv_sem)

    def meet():
        greet([(dp, lax.rem(head + k, 16)) for k in range(1, 16)] + [(dp + 1 - 2 * c, head)] + [
            (lax.rem(z + k, 8) * 2 + c, head) for k in range(1, 8)])

    make_kv(place, copies, st_ref, gain_ref, w_any, bias_ref, kv_ref, w_ref, sq_ref, n_ref, part_ref, own_ref,
            recv_ref, recv2_ref, w_sem, meet)
    make_corr(place, copies, kv_ref, sketch_ref, whole_ref, gpart_ref, half_ref, z_ref, g_ref)
    iterate(place, g_ref, whole_ref, kv_ref, basis_ref, latent_ref, cols_ref, q_ref, pair_ref, panel_send, panel_recv)
    copies.finish()


def local(states, gain, kv_weight, kv_bias, sketch):
    n = 15 + 4 * 12 + 13 + 8 + 14
    return pl.pallas_call(
        kernel,
        out_shape=(jax.ShapeDtypeStruct((128, 512), F32), jax.ShapeDtypeStruct((512, 32), F32)),
        in_specs=[VM, VM, pl.BlockSpec(memory_space=pl.ANY), VM, VM],
        out_specs=(VM, VM),
        scratch_shapes=[
            pltpu.VMEM((4, 4, 512, 128), BF16),
            pltpu.VMEM((512, 2048), BF16),
            pltpu.VMEM((16, 8, 512), F32),
            pltpu.VMEM((512, 512), BF16),
            pltpu.VMEM((4, 4, 512, 128), BF16),
            pltpu.VMEM((4, 4, 128, 128), F32),
            pltpu.VMEM((4, 3, 4, 128, 128), BF16),
            pltpu.VMEM((4, 3, 128, 128), F32),
            pltpu.VMEM((4, 4, 128, 512), BF16),
            pltpu.VMEM((2, 8, 64, 256), F32),
            pltpu.VMEM((8, 64, 256), F32),
            pltpu.VMEM((7, 64, 256), F32),
            pltpu.VMEM((64, 2048), F32),
            pltpu.VMEM((12, 4, 4, 128, 256), BF16),
            pltpu.VMEM((12, 2048, 256), BF16),
            pltpu.VMEM((128, 2048), BF16),
            DMA,
            DMA((n,)),
            DMA((n,)),
            DMA((12, 13)),
            DMA((12, 13)),
        ],
        compiler_params=pltpu.CompilerParams(collective_id=1, has_side_effects=True, vmem_limit_bytes=60 << 20),
    )(states, gain.reshape(1, 512), kv_weight, kv_bias.reshape(1, 128), sketch)


def solution(mesh):
    in_specs = (P("dp", "head"), P("head"), P("head", None), P("head"), P("head", None))
    out_specs = (P("head", None), P("dp", "head"))
    return jax.shard_map(local, mesh=mesh, in_specs=in_specs, out_specs=out_specs, check_vma=False)
```

```python
import jax
import jax.numpy as jnp
from jax import lax
from jax.experimental import pallas as pl
from jax.experimental.pallas import tpu as pltpu
from jax.sharding import PartitionSpec as P

D = 8192
F32 = jnp.float32
BF16 = jnp.bfloat16
MESH = pl.DeviceIdType.MESH
VM = pl.BlockSpec(memory_space=pltpu.VMEM)
DMA = pltpu.SemaphoreType.DMA


def position():
    dp, head = lax.axis_index("dp"), lax.axis_index("head")
    return dp, head, dp // 2, dp % 2, head // 4, head % 4


def greet(devices):
    barrier = pltpu.get_barrier_semaphore()
    for device in devices:
        pl.semaphore_signal(barrier, inc=1, device_id=device, device_id_type=MESH)
    pl.semaphore_wait(barrier, len(devices))


class Copies:
    def __init__(self, send_sem, recv_sem):
        self.send_sem, self.recv_sem, self.started = send_sem, recv_sem, []

    def go(self, src, dst, device):
        n = len(self.started)
        copy = pltpu.make_async_remote_copy(
            src_ref=src, dst_ref=dst, send_sem=self.send_sem.at[n],
            recv_sem=self.recv_sem.at[n], device_id=device, device_id_type=MESH,
        )
        copy.start()
        self.started.append(copy)
        return copy

    def finish(self):
        for copy in self.started:
            copy.wait_send()


def dot(a, b, dims, precision=None):
    return lax.dot_general(a, b, (dims, ((), ())), precision=precision, preferred_element_type=F32)


NN, NT, TN = ((1,), (0,)), ((1,), (1,)), ((0,), (0,))
HI = lax.Precision.HIGHEST


def split(v):
    high = v.astype(BF16)
    return high, (v - high.astype(F32)).astype(BF16)


def make_kv(place, copies, st_ref, gain_ref, w_any, bias_ref, sketch_ref, kv_ref, w_ref, sq_ref, n_ref, part_ref,
            own_ref, recv_ref, recv2_ref, whole_ref, w_sem, meet):
    dp, head, _, c, y, x = place
    half = pl.ds(pl.multiple_of(c * 64, 64), 64)
    part_a = pl.ds(pl.multiple_of(c * 64, 32), 32)
    part_b = pl.ds(pl.multiple_of(c * 64 + 32, 32), 32)
    whole_ref[y, x, half] = sketch_ref[half].astype(BF16)
    load = pltpu.make_async_copy(w_any, w_ref, w_sem)
    load.start()
    others = [lax.rem(head + k, 16) for k in range(1, 16)]
    xs = [lax.rem(x + k, 4) for k in (2, 1, 3)]
    ys = [lax.rem(y + k, 4) for k in (2, 1, 3)]
    to_x = [(dp, y * 4 + v) for v in xs]
    to_y = [(dp, v * 4 + x) for v in ys]

    values = st_ref[...].astype(F32)
    high, low = split(values * values)
    ones = jnp.ones((16, 512), BF16)
    sq_ref[head] = (dot(ones, high, NT) + dot(ones, low, NT))[:8]
    meet()
    arrivals = [copies.go(sq_ref.at[head, 0:1], sq_ref.at[head, 0:1], (dp, v)) for v in others]
    spread = [copies.go(whole_ref.at[y, x, part_a], whole_ref.at[y, x, part_a], d) for d in to_x]
    spread += [copies.go(whole_ref.at[y, x, part_b], whole_ref.at[y, x, part_b], d) for d in to_y]
    for copy in arrivals:
        copy.wait_recv()
    total = sq_ref[0, 0:1]
    for k in range(1, 16):
        total = total + sq_ref[k, 0:1]
    scale = lax.rsqrt(total / D + 1e-06)
    column = jnp.transpose(jnp.broadcast_to(scale, (128, 512)))
    for block in range(4):
        cols = pl.ds(128 * block, 128)
        part = st_ref[:, cols].astype(F32) * column * gain_ref[:, cols]
        n_ref[:, cols] = part.astype(BF16)
    load.wait()

    def product(rows, owner):
        cols = pl.ds(pl.multiple_of(owner * 128, 128), 128)
        return dot(n_ref[rows], w_ref[:, cols], NN)

    for copy in spread:
        copy.wait_recv()
    spread = [copies.go(whole_ref.at[y, :, part_a], whole_ref.at[y, :, part_a], d) for d in to_y]
    spread += [copies.go(whole_ref.at[:, x, part_b], whole_ref.at[:, x, part_b], d) for d in to_x]
    chunks = [pl.ds(128 * n, 128) for n in range(4)]
    first = [[], [], [], []]
    for k in range(3):
        for v in range(4):
            part_ref[v, xs[k]] = product(pl.ds(0, 512), v * 4 + xs[k]).astype(BF16)
        for n in range(2):
            first[n].append(copies.go(part_ref.at[:, xs[k], chunks[n]], recv_ref.at[n, k], to_x[k]))
    for v in range(4):
        whole = product(pl.ds(0, 512), v * 4 + x)
        part_ref[v, x] = whole.astype(BF16)
        own_ref[0, v] = whole[:128]
        own_ref[1, v] = whole[128:256]
    for n in range(2, 4):
        for k in range(3):
            first[n].append(copies.go(part_ref.at[ys[k], :, chunks[n]], recv_ref.at[n, k], to_y[k]))
    for v in range(4):
        own = product(pl.ds(256, 256), y * 4 + v)
        own_ref[2, v] = own[:128]
        own_ref[3, v] = own[128:]
    sequence = (0, 2, 1, 3)
    second = [None] * 4
    for n in sequence:
        for copy in first[n]:
            copy.wait_recv()
        for v in range(4):
            own_ref[n, v] += (recv_ref[n, 0, v].astype(F32) + recv_ref[n, 1, v].astype(F32)) + recv_ref[
                n, 2, v].astype(F32)
        far, to = (ys, to_y) if n < 2 else (xs, to_x)
        second[n] = [copies.go(own_ref.at[n, far[k]], recv2_ref.at[n, k], to[k]) for k in range(3)]
    for copy in spread:
        copy.wait_recv()
    spread = copies.go(whole_ref.at[:, :, half], whole_ref.at[:, :, half], (dp + 1 - 2 * c, head))
    third = [None] * 4
    for n in sequence:
        for copy in second[n]:
            copy.wait_recv()
        summed = own_ref[n, y if n < 2 else x] + (recv2_ref[n, 0] + recv2_ref[n, 1]) + recv2_ref[n, 2]
        kv_ref[y, x, chunks[n]] = (summed + bias_ref[...]).astype(BF16)
        block = kv_ref.at[y, x, chunks[n]]
        third[n] = [copies.go(block, block, d) for d in (to_x if n < 2 else to_y)]
    fourth = []
    for n in sequence:
        for copy in third[n]:
            copy.wait_recv()
        line = kv_ref.at[y, :, chunks[n]] if n < 2 else kv_ref.at[:, x, chunks[n]]
        fourth += [copies.go(line, line, d) for d in (to_y if n < 2 else to_x)]
    for copy in fourth + [spread]:
        copy.wait_recv()


class Corr:
    def __init__(self, place, copies, kv_ref, part, recv_half, recv_z, g_ref):
        dp, head, z, c, y, x = place
        self.copies, self.z, self.c = copies, z, c
        self.part, self.recv_half, self.recv_z, self.g_ref = part, recv_half, recv_z, g_ref
        self.sibling = (dp + 1 - 2 * c, head)
        self.zs = [lax.rem(z + k, 8) for k in (4, 3, 5, 2, 6, 1, 7)]
        self.to_z = [(v * 2 + c, head) for v in self.zs]

    def terms(self, kv_ref, mine):
        for owner in range(8):
            pair = [kv_ref[owner // 2, owner % 2 * 2 + n] for n in range(2)]
            value = dot(mine, jnp.concatenate(pair, axis=1), TN)
            self.part[0, owner] = value[:64]
            self.part[1, owner] = value[64:]
        self.swaps = [
            self.copies.go(self.part.at[1 - self.c, v], self.recv_half.at[v], self.sibling) for v in self.zs + [self.z]]

    def swapped(self):
        self.first = []
        for k in range(7):
            v = self.zs[k]
            self.swaps[k].wait_recv()
            self.part[self.c, v] += self.recv_half[v]
            self.first.append(self.copies.go(self.part.at[self.c, v], self.recv_z.at[k], self.to_z[k]))
        self.swaps[7].wait_recv()

    def summed(self):
        total = self.part[self.c, self.z] + self.recv_half[self.z]
        for k in range(7):
            self.first[k].wait_recv()
            total = total + self.recv_z[k]
        cols = pl.ds(pl.multiple_of(self.z * 256, 256), 256)
        self.g_ref[:, cols] = total
        self.second = [self.copies.go(self.g_ref.at[:, cols], self.g_ref.at[:, cols], d) for d in self.to_z]

    def gathered(self):
        for copy in self.second:
            copy.wait_recv()


def first_columns(place, copies, corr, kv_ref, whole_ref, cpart_ref, chalf_ref, cz_ref, c0_ref):
    dp, head, z, c, y, x = place
    mine = kv_ref[y, x]
    products = jnp.zeros((512, 512), F32)
    for owner in range(8):
        pair = [kv_ref[owner // 2, owner % 2 * 2 + n] for n in range(2)]
        there = [whole_ref[owner // 2, owner % 2 * 2 + n] for n in range(2)]
        products = products + dot(jnp.concatenate(pair, axis=1), jnp.concatenate(there, axis=0), NN)
    high, low = split(products)
    value = dot(mine, high, TN) + dot(mine, low, TN)
    cpart_ref[0] = value[:64]
    cpart_ref[1] = value[64:]
    swap = copies.go(cpart_ref.at[1 - c], chalf_ref, corr.sibling)
    corr.terms(kv_ref, mine)
    swap.wait_recv()
    cpart_ref[c] += chalf_ref[...]

    def rows(owner):
        return pl.ds(pl.multiple_of(owner * 8, 8), 8)

    first = [copies.go(cpart_ref.at[c, rows(corr.zs[k])], cz_ref.at[k], corr.to_z[k]) for k in range(7)]
    total = cpart_ref[c, rows(z)]
    for k in range(7):
        first[k].wait_recv()
        total = total + cz_ref[k]
    c0_ref[rows(z)] = total
    second = [copies.go(c0_ref.at[rows(z)], c0_ref.at[rows(z)], d) for d in corr.to_z]
    corr.swapped()
    for copy in second:
        copy.wait_recv()


def invert_block(a):
    shape = (8, 128)
    rows = [a[8 * g:8 * g + 8] for g in range(16)]
    lane = lax.broadcasted_iota(jnp.int32, shape, 1)
    sub = lax.broadcasted_iota(jnp.int32, shape, 0)
    inverse = [(lane == sub + 8 * g).astype(F32) for g in range(16)]
    for p in range(16):
        spread = [[jnp.broadcast_to(rows[g][:, 8 * p + c:8 * p + c + 1], shape) for g in range(p, 16)]
                  for c in range(8)]
        pivots = None
        for r in range(8):
            pivot = jnp.broadcast_to(spread[r][0][r:r + 1], shape)
            pivots = pivot if pivots is None else jnp.where(sub == r, pivot, pivots)
            recip = 1.0 / pivot
            row = jnp.broadcast_to(rows[p][r:r + 1], shape) * recip
            inverse_row = jnp.broadcast_to(inverse[p][r:r + 1], shape) * recip
            heads = {c: jnp.broadcast_to(spread[c][0][r:r + 1], shape) * recip for c in range(r + 1, 8)}
            for i in range(16 - p):
                if i == 0 and r == 7:
                    continue
                factor = spread[r][i]
                if i == 0:
                    factor = jnp.where(sub > r, factor, 0.0)
                for c in range(r + 1, 8):
                    spread[c][i] = spread[c][i] - factor * heads[c]
                rows[p + i] = rows[p + i] - factor * row
                inverse[p + i] = inverse[p + i] - factor * inverse_row
        inverse[p] = inverse[p] * lax.rsqrt(pivots)
    return jnp.concatenate(inverse, axis=0)


def order(t):
    r = t % 4
    return t + (r // 3) * (1 - t // 11) - (1 - (r + 3) // 4) * ((t + 11) // 12)


def beside(v):
    return jnp.concatenate(split(v), axis=1)


def halves(v):
    return v[:, :128] + v[:, 128:]


def quarters(v):
    rows = v.shape[0] // 2
    return halves(v[:rows]) + halves(v[rows:])


def iterate(place, corr, c0_ref, kv_ref, basis_ref, latent_ref, cols_ref, q_ref, pair_ref, total_ref, send_sem,
            recv_sem):
    dp, head, _, c, y, x = place
    xs = [lax.rem(x + k, 4) for k in (1, 2, 3)]
    ys = [lax.rem(y + k, 4) for k in (1, 2, 3)]
    to_x = [(dp, y * 4 + v) for v in xs]
    to_y = [(dp, v * 4 + x) for v in ys]
    sibling = (dp + 1 - 2 * c, head)
    half = pl.ds(pl.multiple_of(c * 64, 64), 64)
    part_a = pl.ds(pl.multiple_of(c * 64, 32), 32)
    part_b = pl.ds(pl.multiple_of(c * 64 + 32, 32), 32)

    def copy(kp, n, where, device):
        here = cols_ref.at[(kp,) + where]
        return pltpu.make_async_remote_copy(
            src_ref=here, dst_ref=here, send_sem=send_sem.at[kp, n], recv_sem=recv_sem.at[kp, n],
            device_id=device, device_id_type=MESH,
        )

    every = slice(None)

    def first(kp):
        return [copy(kp, n, (y, x, part_a), to_x[n]) for n in range(3)] + [
            copy(kp, 3 + n, (y, x, part_b), to_y[n]) for n in range(3)]

    def second(kp):
        return [copy(kp, 6 + n, (y, every, part_a), to_y[n]) for n in range(3)] + [
            copy(kp, 9 + n, (every, x, part_b), to_x[n]) for n in range(3)]

    def third(kp):
        return [copy(kp, 12, (every, every, half), sibling)]

    def go(some):
        for one in some:
            one.start()

    def arrive(some):
        for one in some:
            one.wait_recv()

    def leave(some):
        for one in some:
            one.wait_send()

    for p in range(4):
        cols_ref[p, y, x, half] = beside(c0_ref[:, 128 * p:128 * p + 128])
        go(first(p))
    for p in range(4):
        arrive(first(p))
        go(second(p))
    arrive(second(0))
    go(third(0))
    corr.summed()

    def task(t, carry):
        kp = order(t)
        k, p = kp // 4, kp % 4
        arrive(third(kp))
        leave(first(kp) + second(kp) + third(kp))

        for n in range(1, 4):
            @pl.when(p == n)
            def _():
                now = cols_ref[kp].reshape(2048, 256)
                factors = [beside(quarters(dot(q_ref[k * 4 + q], now, TN))) for q in range(n)]
                weights = [jnp.concatenate([factor, factor], axis=0) for factor in factors]
                taken = dot(q_ref[k * 4], weights[0], NN)
                for q in range(1, n):
                    taken = taken + dot(q_ref[k * 4 + q], weights[q], NN)
                cols_ref[kp] = beside(halves(now.astype(F32)) - halves(taken)).reshape(4, 4, 128, 256)

        @pl.when(t < 3)
        def _():
            arrive(second(t + 1))
            go(third(t + 1))

        now = cols_ref[kp].reshape(2048, 256)
        block = invert_block(quarters(dot(now, now, TN)))

        @pl.when((t >= 2) & (order(t - 2 + 2 * (1 - (t + 10) // 12)) < 8))
        def _():
            due = order(t - 2) + 4
            arrive(second(due))
            go(third(due))

        @pl.when((t >= 1) & (order(t - 1 + (1 - (t + 11) // 12)) < 8))
        def _():
            due = order(t - 1) + 4
            arrive(first(due))
            go(second(due))

        high, low = split(block)
        weights = jnp.concatenate(
            [jnp.concatenate([high, high], axis=1), jnp.concatenate([low, low], axis=1)], axis=0)
        for r in range(4):
            rows = pl.ds(512 * r, 512)
            q_ref[kp, rows] = beside(halves(dot(cols_ref[kp, r].reshape(512, 256), weights, NT)))

        @pl.when(t == 0)
        def _():
            corr.gathered()
            pair_ref[:64], pair_ref[64:] = split(corr.g_ref[...])

        @pl.when(k < 2)
        def _():
            cols_ref[kp + 4, y, x, half] = beside(quarters(dot(pair_ref[...], q_ref[kp], NN)))
            go(first(kp + 4))

        @pl.when(k == 2)
        def _():
            rows = pl.ds(pl.multiple_of(head * 128, 128), 128)
            basis_ref[:, pl.ds(pl.multiple_of(p * 128, 128), 128)] = halves(q_ref[kp, rows].astype(F32))

        return carry

    lax.fori_loop(0, 12, task, 0)
    total = jnp.zeros((512, 256), F32)
    for owner in range(8):
        pair = [kv_ref[owner // 2, owner % 2 * 2 + n] for n in range(2)]
        there = q_ref[8 + head // 4, 256 * owner:256 * owner + 256]
        total = total + dot(jnp.concatenate(pair, axis=1), there, NN)
    total_ref[...] = jnp.transpose(halves(total))
    latent_ref[...] = total_ref[pl.ds(pl.multiple_of(head % 4 * 32, 32), 32), :]


def kernel(st_ref, gain_ref, w_any, bias_ref, sketch_ref, basis_ref, latent_ref, kv_ref, w_ref, sq_ref, n_ref,
           part_ref, own_ref, recv_ref, recv2_ref, whole_ref, gpart_ref, half_ref, z_ref, g_ref, cpart_ref, chalf_ref,
           cz_ref, c0_ref, cols_ref, q_ref, pair_ref, total_ref, w_sem, send_sem, recv_sem, panel_send, panel_recv):
    place = position()
    dp, head, z, c, _, _ = place
    copies = Copies(send_sem, recv_sem)

    def meet():
        greet([(dp, lax.rem(head + k, 16)) for k in range(1, 16)] + [(dp + 1 - 2 * c, head)] + [
            (lax.rem(z + k, 8) * 2 + c, head) for k in range(1, 8)])

    make_kv(place, copies, st_ref, gain_ref, w_any, bias_ref, sketch_ref, kv_ref, w_ref, sq_ref, n_ref, part_ref,
            own_ref, recv_ref, recv2_ref, whole_ref, w_sem, meet)
    corr = Corr(place, copies, kv_ref, gpart_ref, half_ref, z_ref, g_ref)
    first_columns(place, copies, corr, kv_ref, whole_ref, cpart_ref, chalf_ref, cz_ref, c0_ref)
    iterate(place, corr, c0_ref, kv_ref, basis_ref, latent_ref, cols_ref, q_ref, pair_ref, total_ref, panel_send,
            panel_recv)
    copies.finish()


def finish_kernel(basis_ref, latent_ref, basis_out, latent_out):
    basis_out[...] = basis_ref[...]
    latent_out[...] = latent_ref[...]


def local(states, gain, kv_weight, kv_bias, sketch):
    n = 15 + 4 * 12 + 13 + 8 + 14 + 15
    shapes = (jax.ShapeDtypeStruct((128, 512), F32), jax.ShapeDtypeStruct((32, 512), F32))
    basis, latent = pl.pallas_call(
        kernel,
        out_shape=shapes,
        in_specs=[VM, VM, pl.BlockSpec(memory_space=pl.ANY), VM, VM],
        out_specs=(VM, VM),
        scratch_shapes=[
            pltpu.VMEM((4, 4, 512, 128), BF16),
            pltpu.VMEM((512, 2048), BF16),
            pltpu.VMEM((16, 8, 512), F32),
            pltpu.VMEM((512, 512), BF16),
            pltpu.VMEM((4, 4, 512, 128), BF16),
            pltpu.VMEM((4, 4, 128, 128), F32),
            pltpu.VMEM((4, 3, 4, 128, 128), BF16),
            pltpu.VMEM((4, 3, 128, 128), F32),
            pltpu.VMEM((4, 4, 128, 512), BF16),
            pltpu.VMEM((2, 8, 64, 256), F32),
            pltpu.VMEM((8, 64, 256), F32),
            pltpu.VMEM((7, 64, 256), F32),
            pltpu.VMEM((64, 2048), F32),
            pltpu.VMEM((2, 64, 512), F32),
            pltpu.VMEM((64, 512), F32),
            pltpu.VMEM((7, 8, 512), F32),
            pltpu.VMEM((64, 512), F32),
            pltpu.VMEM((12, 4, 4, 128, 256), BF16),
            pltpu.VMEM((12, 2048, 256), BF16),
            pltpu.VMEM((128, 2048), BF16),
            pltpu.VMEM((128, 512), F32),
            DMA,
            DMA((n,)),
            DMA((n,)),
            DMA((12, 13)),
            DMA((12, 13)),
        ],
        compiler_params=pltpu.CompilerParams(collective_id=1, has_side_effects=True, vmem_limit_bytes=60 << 20),
    )(states, gain.reshape(1, 512), kv_weight, kv_bias.reshape(1, 128), sketch)
    basis, latent = pl.pallas_call(finish_kernel, out_shape=shapes, in_specs=[VM] * 2, out_specs=(VM, VM))(basis, latent)
    return basis, latent.T


def solution(mesh):
    in_specs = (P("dp", "head"), P("head"), P("head", None), P("head"), P("head", None))
    out_specs = (P("head", None), P("dp", "head"))
    return jax.shard_map(local, mesh=mesh, in_specs=in_specs, out_specs=out_specs, check_vma=False)
```

```python
import jax
import jax.numpy as jnp
from jax import lax
from jax.experimental import pallas as pl
from jax.experimental.pallas import tpu as pltpu
from jax.sharding import PartitionSpec as P

D = 8192
F32 = jnp.float32
BF16 = jnp.bfloat16
MESH = pl.DeviceIdType.MESH
VM = pl.BlockSpec(memory_space=pltpu.VMEM)
DMA = pltpu.SemaphoreType.DMA


def position():
    dp, head = lax.axis_index("dp"), lax.axis_index("head")
    return dp, head, dp // 2, dp % 2, head // 4, head % 4


def greet(devices):
    barrier = pltpu.get_barrier_semaphore()
    for device in devices:
        pl.semaphore_signal(barrier, inc=1, device_id=device, device_id_type=MESH)
    pl.semaphore_wait(barrier, len(devices))


class Copies:
    def __init__(self, send_sem, recv_sem):
        self.send_sem, self.recv_sem, self.started = send_sem, recv_sem, []

    def go(self, src, dst, device):
        n = len(self.started)
        copy = pltpu.make_async_remote_copy(
            src_ref=src, dst_ref=dst, send_sem=self.send_sem.at[n],
            recv_sem=self.recv_sem.at[n], device_id=device, device_id_type=MESH,
        )
        copy.start()
        self.started.append(copy)
        return copy

    def finish(self):
        for copy in self.started:
            copy.wait_send()


def dot(a, b, dims, precision=None):
    return lax.dot_general(a, b, (dims, ((), ())), precision=precision, preferred_element_type=F32)


NN, NT, TN = ((1,), (0,)), ((1,), (1,)), ((0,), (0,))
HI = lax.Precision.HIGHEST


def split(v):
    high = v.astype(BF16)
    return high, (v - high.astype(F32)).astype(BF16)


def make_kv(place, copies, st_ref, gain_ref, w_any, bias_ref, sketch_ref, kv_ref, w_ref, sq_ref, n_ref, part_ref,
            own_ref, recv_ref, recv2_ref, whole_ref, w_sem, meet):
    dp, head, _, c, y, x = place
    half = pl.ds(pl.multiple_of(c * 64, 64), 64)
    part_a = pl.ds(pl.multiple_of(c * 64, 32), 32)
    part_b = pl.ds(pl.multiple_of(c * 64 + 32, 32), 32)
    whole_ref[y, x, half] = sketch_ref[half].astype(BF16)
    load = pltpu.make_async_copy(w_any, w_ref, w_sem)
    load.start()
    others = [lax.rem(head + k, 16) for k in range(1, 16)]
    xs = [lax.rem(x + k, 4) for k in (2, 1, 3)]
    ys = [lax.rem(y + k, 4) for k in (2, 1, 3)]
    to_x = [(dp, y * 4 + v) for v in xs]
    to_y = [(dp, v * 4 + x) for v in ys]

    values = st_ref[...].astype(F32)
    high, low = split(values * values)
    ones = jnp.ones((16, 512), BF16)
    squares = dot(ones, high, NT) + dot(ones, low, NT)
    for n in range(4):
        line = squares[0:8, 128 * n:128 * n + 128]
        tile = line if n == 0 else jnp.where(lax.broadcasted_iota(jnp.int32, (8, 128), 0) == n, line, tile)
    sq_ref[head] = tile
    meet()
    arrivals = [copies.go(sq_ref.at[head], sq_ref.at[head], (dp, v)) for v in others]
    spread = [copies.go(whole_ref.at[y, x, part_a], whole_ref.at[y, x, part_a], d) for d in to_x]
    spread += [copies.go(whole_ref.at[y, x, part_b], whole_ref.at[y, x, part_b], d) for d in to_y]
    for copy in arrivals:
        copy.wait_recv()
    total = sq_ref[0]
    for k in range(1, 16):
        total = total + sq_ref[k]
    scale = lax.rsqrt(total / D + 1e-06)
    column = jnp.concatenate(
        [jnp.transpose(jnp.broadcast_to(scale[n:n + 1], (128, 128))) for n in range(4)], axis=0)
    for block in range(4):
        cols = pl.ds(128 * block, 128)
        part = st_ref[:, cols].astype(F32) * column * gain_ref[:, cols]
        n_ref[:, cols] = part.astype(BF16)
    load.wait()

    def product(rows, owner):
        cols = pl.ds(pl.multiple_of(owner * 128, 128), 128)
        return dot(n_ref[rows], w_ref[:, cols], NN)

    for copy in spread:
        copy.wait_recv()
    spread = [copies.go(whole_ref.at[y, :, part_a], whole_ref.at[y, :, part_a], d) for d in to_y]
    spread += [copies.go(whole_ref.at[:, x, part_b], whole_ref.at[:, x, part_b], d) for d in to_x]
    chunks = [pl.ds(128 * n, 128) for n in range(4)]
    first = [[], [], [], []]
    for k in range(3):
        for v in range(4):
            part_ref[v, xs[k]] = product(pl.ds(0, 512), v * 4 + xs[k]).astype(BF16)
        for n in range(2):
            first[n].append(copies.go(part_ref.at[:, xs[k], chunks[n]], recv_ref.at[n, k], to_x[k]))
    for v in range(4):
        whole = product(pl.ds(0, 512), v * 4 + x)
        part_ref[v, x] = whole.astype(BF16)
        own_ref[0, v] = whole[:128]
        own_ref[1, v] = whole[128:256]
    for n in range(2, 4):
        for k in range(3):
            first[n].append(copies.go(part_ref.at[ys[k], :, chunks[n]], recv_ref.at[n, k], to_y[k]))
    for v in range(4):
        own = product(pl.ds(256, 256), y * 4 + v)
        own_ref[2, v] = own[:128]
        own_ref[3, v] = own[128:]
    sequence = (0, 2, 1, 3)
    second = [None] * 4
    for n in sequence:
        for copy in first[n]:
            copy.wait_recv()
        for v in range(4):
            own_ref[n, v] += (recv_ref[n, 0, v].astype(F32) + recv_ref[n, 1, v].astype(F32)) + recv_ref[
                n, 2, v].astype(F32)
        far, to = (ys, to_y) if n < 2 else (xs, to_x)
        second[n] = [copies.go(own_ref.at[n, far[k]], recv2_ref.at[n, k], to[k]) for k in range(3)]
    for copy in spread:
        copy.wait_recv()
    spread = copies.go(whole_ref.at[:, :, half], whole_ref.at[:, :, half], (dp + 1 - 2 * c, head))
    third = [None] * 4
    for n in sequence:
        for copy in second[n]:
            copy.wait_recv()
        summed = own_ref[n, y if n < 2 else x] + (recv2_ref[n, 0] + recv2_ref[n, 1]) + recv2_ref[n, 2]
        kv_ref[y, x, chunks[n]] = (summed + bias_ref[...]).astype(BF16)
        block = kv_ref.at[y, x, chunks[n]]
        third[n] = [copies.go(block, block, d) for d in (to_x if n < 2 else to_y)]
    fourth = [None] * 4
    for n in sequence:
        for copy in third[n]:
            copy.wait_recv()
        line = kv_ref.at[y, :, chunks[n]] if n < 2 else kv_ref.at[:, x, chunks[n]]
        fourth[n] = [copies.go(line, line, d) for d in (to_y if n < 2 else to_x)]
    spread.wait_recv()
    return sequence, fourth


class Corr:
    def __init__(self, place, copies, kv_ref, part, recv_half, recv_z, g_ref):
        dp, head, z, c, y, x = place
        self.copies, self.z, self.c = copies, z, c
        self.part, self.recv_half, self.recv_z, self.g_ref = part, recv_half, recv_z, g_ref
        self.sibling = (dp + 1 - 2 * c, head)
        self.zs = [lax.rem(z + k, 8) for k in (4, 3, 5, 2, 6, 1, 7)]
        self.to_z = [(v * 2 + c, head) for v in self.zs]

    def terms(self, kv_ref, mine):
        for owner in range(8):
            pair = [kv_ref[owner // 2, owner % 2 * 2 + n] for n in range(2)]
            value = dot(mine, jnp.concatenate(pair, axis=1), TN)
            self.part[0, owner] = value[:64]
            self.part[1, owner] = value[64:]
        self.swaps = [
            self.copies.go(self.part.at[1 - self.c, v], self.recv_half.at[v], self.sibling) for v in self.zs + [self.z]]

    def swapped(self):
        self.first = []
        for k in range(7):
            v = self.zs[k]
            self.swaps[k].wait_recv()
            self.part[self.c, v] += self.recv_half[v]
            self.first.append(self.copies.go(self.part.at[self.c, v], self.recv_z.at[k], self.to_z[k]))
        self.swaps[7].wait_recv()

    def summed(self):
        total = self.part[self.c, self.z] + self.recv_half[self.z]
        for k in range(7):
            self.first[k].wait_recv()
            total = total + self.recv_z[k]
        cols = pl.ds(pl.multiple_of(self.z * 256, 256), 256)
        self.g_ref[:, cols] = total
        self.second = [self.copies.go(self.g_ref.at[:, cols], self.g_ref.at[:, cols], d) for d in self.to_z]

    def gathered(self):
        for copy in self.second:
            copy.wait_recv()


def first_columns(place, copies, corr, sequence, arrivals, kv_ref, whole_ref, cpart_ref, chalf_ref, cz_ref, c0_ref):
    dp, head, z, c, y, x = place
    value = jnp.zeros((128, 512), F32)
    for n in sequence:
        for copy in arrivals[n]:
            copy.wait_recv()
        rows = pl.ds(128 * n, 128)
        products = jnp.zeros((128, 512), F32)
        for owner in range(8):
            pair = [kv_ref[owner // 2, owner % 2 * 2 + n, rows] for n in range(2)]
            there = [whole_ref[owner // 2, owner % 2 * 2 + n] for n in range(2)]
            products = products + dot(jnp.concatenate(pair, axis=1), jnp.concatenate(there, axis=0), NN)
        high, low = split(products)
        here = kv_ref[y, x, rows]
        value = value + (dot(here, high, TN) + dot(here, low, TN))
    cpart_ref[0] = value[:64]
    cpart_ref[1] = value[64:]
    swap = copies.go(cpart_ref.at[1 - c], chalf_ref, corr.sibling)
    swap.wait_recv()
    cpart_ref[c] += chalf_ref[...]

    def rows(owner):
        return pl.ds(pl.multiple_of(owner * 8, 8), 8)

    first = [copies.go(cpart_ref.at[c, rows(corr.zs[k])], cz_ref.at[k], corr.to_z[k]) for k in range(7)]
    corr.terms(kv_ref, kv_ref[y, x])
    total = cpart_ref[c, rows(z)]
    for k in range(7):
        first[k].wait_recv()
        total = total + cz_ref[k]
    c0_ref[rows(z)] = total
    second = [copies.go(c0_ref.at[rows(z)], c0_ref.at[rows(z)], d) for d in corr.to_z]
    corr.swapped()
    for copy in second:
        copy.wait_recv()


def invert_block(a):
    shape = (8, 128)
    rows = [a[8 * g:8 * g + 8] for g in range(16)]
    lane = lax.broadcasted_iota(jnp.int32, shape, 1)
    sub = lax.broadcasted_iota(jnp.int32, shape, 0)
    inverse = [(lane == sub + 8 * g).astype(F32) for g in range(16)]
    for p in range(16):
        spread = [[jnp.broadcast_to(rows[g][:, 8 * p + c:8 * p + c + 1], shape) for g in range(p, 16)]
                  for c in range(8)]
        pivots = None
        for r in range(8):
            pivot = jnp.broadcast_to(spread[r][0][r:r + 1], shape)
            pivots = pivot if pivots is None else jnp.where(sub == r, pivot, pivots)
            recip = 1.0 / pivot
            row = jnp.broadcast_to(rows[p][r:r + 1], shape) * recip
            inverse_row = jnp.broadcast_to(inverse[p][r:r + 1], shape) * recip
            heads = {c: jnp.broadcast_to(spread[c][0][r:r + 1], shape) * recip for c in range(r + 1, 8)}
            for i in range(16 - p):
                if i == 0 and r == 7:
                    continue
                factor = spread[r][i]
                if i == 0:
                    factor = jnp.where(sub > r, factor, 0.0)
                for c in range(r + 1, 8):
                    spread[c][i] = spread[c][i] - factor * heads[c]
                rows[p + i] = rows[p + i] - factor * row
                inverse[p + i] = inverse[p + i] - factor * inverse_row
        inverse[p] = inverse[p] * lax.rsqrt(pivots)
    return jnp.concatenate(inverse, axis=0)


def order(t):
    return t + (t // 7) * (1 - t // 8) - (t // 8) * (1 - t // 9)


def beside(v):
    return jnp.concatenate(split(v), axis=1)


def halves(v):
    return v[:, :128] + v[:, 128:]


def quarters(v):
    rows = v.shape[0] // 2
    return halves(v[:rows]) + halves(v[rows:])


def iterate(place, corr, c0_ref, kv_ref, basis_ref, latent_ref, cols_ref, q_ref, pair_ref, total_ref, send_sem,
            recv_sem):
    dp, head, _, c, y, x = place
    xs = [lax.rem(x + k, 4) for k in (1, 2, 3)]
    ys = [lax.rem(y + k, 4) for k in (1, 2, 3)]
    to_x = [(dp, y * 4 + v) for v in xs]
    to_y = [(dp, v * 4 + x) for v in ys]
    sibling = (dp + 1 - 2 * c, head)
    half = pl.ds(pl.multiple_of(c * 64, 64), 64)
    part_a = pl.ds(pl.multiple_of(c * 64, 32), 32)
    part_b = pl.ds(pl.multiple_of(c * 64 + 32, 32), 32)

    def copy(kp, n, where, device):
        here = cols_ref.at[(kp,) + where]
        return pltpu.make_async_remote_copy(
            src_ref=here, dst_ref=here, send_sem=send_sem.at[kp, n], recv_sem=recv_sem.at[kp, n],
            device_id=device, device_id_type=MESH,
        )

    every = slice(None)

    def first(kp):
        return [copy(kp, n, (y, x, part_a), to_x[n]) for n in range(3)] + [
            copy(kp, 3 + n, (y, x, part_b), to_y[n]) for n in range(3)]

    def second(kp):
        return [copy(kp, 6 + n, (y, every, part_a), to_y[n]) for n in range(3)] + [
            copy(kp, 9 + n, (every, x, part_b), to_x[n]) for n in range(3)]

    def third(kp):
        return [copy(kp, 12, (every, every, half), sibling)]

    def go(some):
        for one in some:
            one.start()

    def arrive(some):
        for one in some:
            one.wait_recv()

    def leave(some):
        for one in some:
            one.wait_send()

    for p in range(4):
        cols_ref[p, y, x, half] = beside(c0_ref[:, 128 * p:128 * p + 128])
        go(first(p))
    for p in range(4):
        arrive(first(p))
        go(second(p))
    arrive(second(0))
    go(third(0))
    corr.summed()

    def task(t, carry):
        kp = order(t)
        k, p = kp // 4, kp % 4
        arrive(third(kp))
        leave(first(kp) + second(kp) + third(kp))

        for n in range(1, 4):
            @pl.when(p == n)
            def _():
                now = cols_ref[kp].reshape(2048, 256)
                factors = [beside(quarters(dot(q_ref[k * 4 + q], now, TN))) for q in range(n)]
                weights = [jnp.concatenate([factor, factor], axis=0) for factor in factors]
                taken = dot(q_ref[k * 4], weights[0], NN)
                for q in range(1, n):
                    taken = taken + dot(q_ref[k * 4 + q], weights[q], NN)
                cols_ref[kp] = beside(halves(now.astype(F32)) - halves(taken)).reshape(4, 4, 128, 256)

        @pl.when(t < 3)
        def _():
            arrive(second(t + 1))
            go(third(t + 1))

        now = cols_ref[kp].reshape(2048, 256)
        block = invert_block(quarters(dot(now, now, TN)))

        @pl.when((t >= 3) & (order(t - 2 + 2 * (1 - (t + 10) // 12)) < 8))
        def _():
            due = order(t - 2) + 4
            arrive(second(due))
            go(third(due))

        @pl.when(t == 3)
        def _():
            arrive(second(4))
            go(third(4))

        @pl.when((t >= 2) & (order(t - 1 + (1 - (t + 11) // 12)) < 8))
        def _():
            due = order(t - 1) + 4
            arrive(first(due))
            go(second(due))

        @pl.when(t == 2)
        def _():
            arrive(first(4))
            go(second(4))

        high, low = split(block)
        weights = jnp.concatenate(
            [jnp.concatenate([high, high], axis=1), jnp.concatenate([low, low], axis=1)], axis=0)
        for r in range(4):
            rows = pl.ds(512 * r, 512)
            q_ref[kp, rows] = beside(halves(dot(cols_ref[kp, r].reshape(512, 256), weights, NT)))

        @pl.when(t == 1)
        def _():
            corr.gathered()
            pair_ref[:64], pair_ref[64:] = split(corr.g_ref[...])
            cols_ref[4, y, x, half] = beside(quarters(dot(pair_ref[...], q_ref[0], NN)))
            go(first(4))

        @pl.when((t > 0) & (k < 2))
        def _():
            cols_ref[kp + 4, y, x, half] = beside(quarters(dot(pair_ref[...], q_ref[kp], NN)))
            go(first(kp + 4))

        @pl.when(k == 2)
        def _():
            rows = pl.ds(pl.multiple_of(head * 128, 128), 128)
            basis_ref[:, pl.ds(pl.multiple_of(p * 128, 128), 128)] = halves(q_ref[kp, rows].astype(F32))

        return carry

    lax.fori_loop(0, 12, task, 0)
    total = jnp.zeros((512, 256), F32)
    for owner in range(8):
        pair = [kv_ref[owner // 2, owner % 2 * 2 + n] for n in range(2)]
        there = q_ref[8 + head // 4, 256 * owner:256 * owner + 256]
        total = total + dot(jnp.concatenate(pair, axis=1), there, NN)
    total_ref[...] = jnp.transpose(halves(total))
    latent_ref[...] = total_ref[pl.ds(pl.multiple_of(head % 4 * 32, 32), 32), :]


def kernel(st_ref, gain_ref, w_any, bias_ref, sketch_ref, basis_ref, latent_ref, kv_ref, w_ref, sq_ref, n_ref,
           part_ref, own_ref, recv_ref, recv2_ref, whole_ref, gpart_ref, half_ref, z_ref, g_ref, cpart_ref, chalf_ref,
           cz_ref, c0_ref, cols_ref, q_ref, pair_ref, total_ref, w_sem, send_sem, recv_sem, panel_send, panel_recv):
    place = position()
    dp, head, z, c, _, _ = place
    copies = Copies(send_sem, recv_sem)

    def meet():
        greet([(dp, lax.rem(head + k, 16)) for k in range(1, 16)] + [(dp + 1 - 2 * c, head)] + [
            (lax.rem(z + k, 8) * 2 + c, head) for k in range(1, 8)])

    pending = make_kv(place, copies, st_ref, gain_ref, w_any, bias_ref, sketch_ref, kv_ref, w_ref, sq_ref, n_ref, part_ref,
            own_ref, recv_ref, recv2_ref, whole_ref, w_sem, meet)
    corr = Corr(place, copies, kv_ref, gpart_ref, half_ref, z_ref, g_ref)
    first_columns(place, copies, corr, *pending, kv_ref, whole_ref, cpart_ref, chalf_ref, cz_ref, c0_ref)
    iterate(place, corr, c0_ref, kv_ref, basis_ref, latent_ref, cols_ref, q_ref, pair_ref, total_ref, panel_send,
            panel_recv)
    copies.finish()


def finish_kernel(basis_ref, latent_ref, basis_out, latent_out):
    basis_out[...] = basis_ref[...]
    latent_out[...] = latent_ref[...]


def local(states, gain, kv_weight, kv_bias, sketch):
    n = 15 + 4 * 12 + 13 + 8 + 14 + 15
    shapes = (jax.ShapeDtypeStruct((128, 512), F32), jax.ShapeDtypeStruct((32, 512), F32))
    basis, latent = pl.pallas_call(
        kernel,
        out_shape=shapes,
        in_specs=[VM, VM, pl.BlockSpec(memory_space=pl.ANY), VM, VM],
        out_specs=(VM, VM),
        scratch_shapes=[
            pltpu.VMEM((4, 4, 512, 128), BF16),
            pltpu.VMEM((512, 2048), BF16),
            pltpu.VMEM((16, 8, 128), F32),
            pltpu.VMEM((512, 512), BF16),
            pltpu.VMEM((4, 4, 512, 128), BF16),
            pltpu.VMEM((4, 4, 128, 128), F32),
            pltpu.VMEM((4, 3, 4, 128, 128), BF16),
            pltpu.VMEM((4, 3, 128, 128), F32),
            pltpu.VMEM((4, 4, 128, 512), BF16),
            pltpu.VMEM((2, 8, 64, 256), F32),
            pltpu.VMEM((8, 64, 256), F32),
            pltpu.VMEM((7, 64, 256), F32),
            pltpu.VMEM((64, 2048), F32),
            pltpu.VMEM((2, 64, 512), F32),
            pltpu.VMEM((64, 512), F32),
            pltpu.VMEM((7, 8, 512), F32),
            pltpu.VMEM((64, 512), F32),
            pltpu.VMEM((12, 4, 4, 128, 256), BF16),
            pltpu.VMEM((12, 2048, 256), BF16),
            pltpu.VMEM((128, 2048), BF16),
            pltpu.VMEM((128, 512), F32),
            DMA,
            DMA((n,)),
            DMA((n,)),
            DMA((12, 13)),
            DMA((12, 13)),
        ],
        compiler_params=pltpu.CompilerParams(collective_id=1, has_side_effects=True, vmem_limit_bytes=60 << 20),
    )(states, gain.reshape(1, 512), kv_weight, kv_bias.reshape(1, 128), sketch)
    basis, latent = pl.pallas_call(finish_kernel, out_shape=shapes, in_specs=[VM] * 2, out_specs=(VM, VM))(basis, latent)
    return basis, latent.T


def solution(mesh):
    in_specs = (P("dp", "head"), P("head"), P("head", None), P("head"), P("head", None))
    out_specs = (P("head", None), P("dp", "head"))
    return jax.shard_map(local, mesh=mesh, in_specs=in_specs, out_specs=out_specs, check_vma=False)
```

```python
import jax
import jax.numpy as jnp
from jax import lax
from jax.experimental import pallas as pl
from jax.experimental.pallas import tpu as pltpu
from jax.sharding import PartitionSpec as P

D = 8192
F32 = jnp.float32
BF16 = jnp.bfloat16
MESH = pl.DeviceIdType.MESH
VM = pl.BlockSpec(memory_space=pltpu.VMEM)
DMA = pltpu.SemaphoreType.DMA


def position():
    dp, head = lax.axis_index("dp"), lax.axis_index("head")
    return dp, head, dp // 2, dp % 2, head // 4, head % 4


def greet(devices):
    barrier = pltpu.get_barrier_semaphore()
    for device in devices:
        pl.semaphore_signal(barrier, inc=1, device_id=device, device_id_type=MESH)
    pl.semaphore_wait(barrier, len(devices))


class Copies:
    def __init__(self, send_sem, recv_sem):
        self.send_sem, self.recv_sem, self.started = send_sem, recv_sem, []

    def go(self, src, dst, device):
        n = len(self.started)
        copy = pltpu.make_async_remote_copy(
            src_ref=src, dst_ref=dst, send_sem=self.send_sem.at[n],
            recv_sem=self.recv_sem.at[n], device_id=device, device_id_type=MESH,
        )
        copy.start()
        self.started.append(copy)
        return copy

    def finish(self):
        for copy in self.started:
            copy.wait_send()


def dot(a, b, dims, precision=None):
    return lax.dot_general(a, b, (dims, ((), ())), precision=precision, preferred_element_type=F32)


NN, NT, TN = ((1,), (0,)), ((1,), (1,)), ((0,), (0,))
HI = lax.Precision.HIGHEST


def split(v):
    high = v.astype(BF16)
    return high, (v - high.astype(F32)).astype(BF16)


def make_kv(place, copies, st_ref, gain_ref, w_any, bias_ref, sketch_ref, kv_ref, w_ref, sq_ref, n_ref, part_ref,
            own_ref, recv_ref, recv2_ref, whole_ref, w_sem, meet):
    dp, head, _, c, y, x = place
    half = pl.ds(pl.multiple_of(c * 64, 64), 64)
    part_a = pl.ds(pl.multiple_of(c * 64, 32), 32)
    part_b = pl.ds(pl.multiple_of(c * 64 + 32, 32), 32)
    whole_ref[y, x, half] = sketch_ref[half].astype(BF16)
    load = pltpu.make_async_copy(w_any, w_ref, w_sem)
    load.start()
    others = [lax.rem(head + k, 16) for k in range(1, 16)]
    xs = [lax.rem(x + k, 4) for k in (2, 1, 3)]
    ys = [lax.rem(y + k, 4) for k in (2, 1, 3)]
    to_x = [(dp, y * 4 + v) for v in xs]
    to_y = [(dp, v * 4 + x) for v in ys]

    values = st_ref[...].astype(F32)
    high, low = split(values * values)
    ones = jnp.ones((16, 512), BF16)
    squares = dot(ones, high, NT) + dot(ones, low, NT)
    for n in range(4):
        line = squares[0:8, 128 * n:128 * n + 128]
        tile = line if n == 0 else jnp.where(lax.broadcasted_iota(jnp.int32, (8, 128), 0) == n, line, tile)
    sq_ref[head] = tile
    meet()
    arrivals = [copies.go(sq_ref.at[head], sq_ref.at[head], (dp, v)) for v in others]
    spread = [copies.go(whole_ref.at[y, x, part_a], whole_ref.at[y, x, part_a], d) for d in to_x]
    spread += [copies.go(whole_ref.at[y, x, part_b], whole_ref.at[y, x, part_b], d) for d in to_y]
    for copy in arrivals:
        copy.wait_recv()
    total = sq_ref[0]
    for k in range(1, 16):
        total = total + sq_ref[k]
    scale = lax.rsqrt(total / D + 1e-06)
    column = jnp.concatenate(
        [jnp.transpose(jnp.broadcast_to(scale[n:n + 1], (128, 128))) for n in range(4)], axis=0)
    for block in range(4):
        cols = pl.ds(128 * block, 128)
        part = st_ref[:, cols].astype(F32) * column * gain_ref[:, cols]
        n_ref[:, cols] = part.astype(BF16)
    load.wait()

    def product(rows, owner):
        cols = pl.ds(pl.multiple_of(owner * 128, 128), 128)
        return dot(n_ref[rows], w_ref[:, cols], NN)

    for copy in spread:
        copy.wait_recv()
    spread = [copies.go(whole_ref.at[y, :, part_a], whole_ref.at[y, :, part_a], d) for d in to_y]
    spread += [copies.go(whole_ref.at[:, x, part_b], whole_ref.at[:, x, part_b], d) for d in to_x]
    chunks = [pl.ds(128 * n, 128) for n in range(4)]
    first = [[], [], [], []]
    for k in range(3):
        for v in range(4):
            part_ref[v, xs[k]] = product(pl.ds(0, 512), v * 4 + xs[k]).astype(BF16)
        for n in range(2):
            first[n].append(copies.go(part_ref.at[:, xs[k], chunks[n]], recv_ref.at[n, k], to_x[k]))
    for v in range(4):
        whole = product(pl.ds(0, 512), v * 4 + x)
        part_ref[v, x] = whole.astype(BF16)
        own_ref[0, v] = whole[:128]
        own_ref[1, v] = whole[128:256]
    for n in range(2, 4):
        for k in range(3):
            first[n].append(copies.go(part_ref.at[ys[k], :, chunks[n]], recv_ref.at[n, k], to_y[k]))
    for v in range(4):
        own = product(pl.ds(256, 256), y * 4 + v)
        own_ref[2, v] = own[:128]
        own_ref[3, v] = own[128:]
    sequence = (0, 2, 1, 3)
    second = [None] * 4
    for n in sequence:
        for copy in first[n]:
            copy.wait_recv()
        for v in range(4):
            own_ref[n, v] += (recv_ref[n, 0, v].astype(F32) + recv_ref[n, 1, v].astype(F32)) + recv_ref[
                n, 2, v].astype(F32)
        far, to = (ys, to_y) if n < 2 else (xs, to_x)
        second[n] = [copies.go(own_ref.at[n, far[k]], recv2_ref.at[n, k], to[k]) for k in range(3)]
    for copy in spread:
        copy.wait_recv()
    spread = copies.go(whole_ref.at[:, :, half], whole_ref.at[:, :, half], (dp + 1 - 2 * c, head))
    third = [None] * 4
    for n in sequence:
        for copy in second[n]:
            copy.wait_recv()
        summed = own_ref[n, y if n < 2 else x] + (recv2_ref[n, 0] + recv2_ref[n, 1]) + recv2_ref[n, 2]
        kv_ref[y, x, chunks[n]] = (summed + bias_ref[...]).astype(BF16)
        block = kv_ref.at[y, x, chunks[n]]
        third[n] = [copies.go(block, block, d) for d in (to_x if n < 2 else to_y)]
    fourth = [None] * 4
    for n in sequence:
        for copy in third[n]:
            copy.wait_recv()
        line = kv_ref.at[y, :, chunks[n]] if n < 2 else kv_ref.at[:, x, chunks[n]]
        fourth[n] = [copies.go(line, line, d) for d in (to_y if n < 2 else to_x)]
    spread.wait_recv()
    return sequence, fourth


class Corr:
    def __init__(self, place, copies, kv_ref, part, recv_half, recv_z, g_ref):
        dp, head, z, c, y, x = place
        self.copies, self.z, self.c = copies, z, c
        self.part, self.recv_half, self.recv_z, self.g_ref = part, recv_half, recv_z, g_ref
        self.sibling = (dp + 1 - 2 * c, head)
        self.zs = [lax.rem(z + k, 8) for k in (4, 3, 5, 2, 6, 1, 7)]
        self.to_z = [(v * 2 + c, head) for v in self.zs]

    def terms(self, kv_ref, mine):
        for owner in range(8):
            pair = [kv_ref[owner // 2, owner % 2 * 2 + n] for n in range(2)]
            value = dot(mine, jnp.concatenate(pair, axis=1), TN)
            self.part[0, owner] = value[:64]
            self.part[1, owner] = value[64:]
        self.swaps = [
            self.copies.go(self.part.at[1 - self.c, v], self.recv_half.at[v], self.sibling) for v in self.zs + [self.z]]

    def swapped(self):
        self.first = []
        for k in range(7):
            v = self.zs[k]
            self.swaps[k].wait_recv()
            self.part[self.c, v] += self.recv_half[v]
            self.first.append(self.copies.go(self.part.at[self.c, v], self.recv_z.at[k], self.to_z[k]))
        self.swaps[7].wait_recv()

    def summed(self):
        total = self.part[self.c, self.z] + self.recv_half[self.z]
        for k in range(7):
            self.first[k].wait_recv()
            total = total + self.recv_z[k]
        cols = pl.ds(pl.multiple_of(self.z * 256, 256), 256)
        self.g_ref[:, cols] = total
        self.second = [self.copies.go(self.g_ref.at[:, cols], self.g_ref.at[:, cols], d) for d in self.to_z]

    def gathered(self):
        for copy in self.second:
            copy.wait_recv()


def first_columns(place, copies, corr, sequence, arrivals, kv_ref, whole_ref, cpart_ref, chalf_ref, cz_ref, c0_ref):
    dp, head, z, c, y, x = place
    value = jnp.zeros((128, 512), F32)
    for n in sequence:
        for copy in arrivals[n]:
            copy.wait_recv()
        rows = pl.ds(128 * n, 128)
        products = jnp.zeros((128, 512), F32)
        for owner in range(8):
            pair = [kv_ref[owner // 2, owner % 2 * 2 + n, rows] for n in range(2)]
            there = [whole_ref[owner // 2, owner % 2 * 2 + n] for n in range(2)]
            products = products + dot(jnp.concatenate(pair, axis=1), jnp.concatenate(there, axis=0), NN)
        high, low = split(products)
        here = kv_ref[y, x, rows]
        value = value + (dot(here, high, TN) + dot(here, low, TN))
    cpart_ref[0] = value[:64]
    cpart_ref[1] = value[64:]
    swap = copies.go(cpart_ref.at[1 - c], chalf_ref, corr.sibling)
    swap.wait_recv()
    cpart_ref[c] += chalf_ref[...]

    def rows(owner):
        return pl.ds(pl.multiple_of(owner * 8, 8), 8)

    first = [copies.go(cpart_ref.at[c, rows(corr.zs[k])], cz_ref.at[k], corr.to_z[k]) for k in range(7)]
    corr.terms(kv_ref, kv_ref[y, x])
    total = cpart_ref[c, rows(z)]
    for k in range(7):
        first[k].wait_recv()
        total = total + cz_ref[k]
    c0_ref[rows(z)] = total
    second = [copies.go(c0_ref.at[rows(z)], c0_ref.at[rows(z)], d) for d in corr.to_z]
    corr.swapped()
    for copy in second:
        copy.wait_recv()


def invert_block(a):
    shape = (8, 128)
    rows = [a[8 * g:8 * g + 8] for g in range(16)]
    lane = lax.broadcasted_iota(jnp.int32, shape, 1)
    sub = lax.broadcasted_iota(jnp.int32, shape, 0)
    inverse = [(lane == sub + 8 * g).astype(F32) for g in range(16)]
    for p in range(16):
        spread = [[jnp.broadcast_to(rows[g][:, 8 * p + c:8 * p + c + 1], shape) for g in range(p, 16)]
                  for c in range(8)]
        pivots = None
        for r in range(8):
            pivot = jnp.broadcast_to(spread[r][0][r:r + 1], shape)
            pivots = pivot if pivots is None else jnp.where(sub == r, pivot, pivots)
            recip = 1.0 / pivot
            row = jnp.broadcast_to(rows[p][r:r + 1], shape) * recip
            inverse_row = jnp.broadcast_to(inverse[p][r:r + 1], shape) * recip
            heads = {c: jnp.broadcast_to(spread[c][0][r:r + 1], shape) * recip for c in range(r + 1, 8)}
            for i in range(16 - p):
                if i == 0 and r == 7:
                    continue
                factor = spread[r][i]
                if i == 0:
                    factor = jnp.where(sub > r, factor, 0.0)
                for c in range(r + 1, 8):
                    spread[c][i] = spread[c][i] - factor * heads[c]
                rows[p + i] = rows[p + i] - factor * row
                inverse[p + i] = inverse[p + i] - factor * inverse_row
        inverse[p] = inverse[p] * lax.rsqrt(pivots)
    return jnp.concatenate(inverse, axis=0)


def order(t):
    return t + (t // 7) * (1 - t // 8) - (t // 8) * (1 - t // 9)


def beside(v):
    return jnp.concatenate(split(v), axis=1)


def halves(v):
    return v[:, :128] + v[:, 128:]


def quarters(v):
    rows = v.shape[0] // 2
    return halves(v[:rows]) + halves(v[rows:])


def iterate(place, corr, c0_ref, kv_ref, basis_ref, latent_ref, cols_ref, q_ref, pair_ref, total_ref, send_sem,
            recv_sem):
    dp, head, _, c, y, x = place
    xs = [lax.rem(x + k, 4) for k in (1, 2, 3)]
    ys = [lax.rem(y + k, 4) for k in (1, 2, 3)]
    to_x = [(dp, y * 4 + v) for v in xs]
    to_y = [(dp, v * 4 + x) for v in ys]
    sibling = (dp + 1 - 2 * c, head)
    half = pl.ds(pl.multiple_of(c * 64, 64), 64)
    part_a = pl.ds(pl.multiple_of(c * 64, 32), 32)
    part_b = pl.ds(pl.multiple_of(c * 64 + 32, 32), 32)

    def copy(kp, n, where, device):
        here = cols_ref.at[(kp,) + where]
        return pltpu.make_async_remote_copy(
            src_ref=here, dst_ref=here, send_sem=send_sem.at[kp, n], recv_sem=recv_sem.at[kp, n],
            device_id=device, device_id_type=MESH,
        )

    every = slice(None)

    def first(kp):
        return [copy(kp, n, (y, x, part_a), to_x[n]) for n in range(3)] + [
            copy(kp, 3 + n, (y, x, part_b), to_y[n]) for n in range(3)]

    def second(kp):
        return [copy(kp, 6 + n, (y, every, part_a), to_y[n]) for n in range(3)] + [
            copy(kp, 9 + n, (every, x, part_b), to_x[n]) for n in range(3)]

    def third(kp):
        return [copy(kp, 12, (every, every, half), sibling)]

    def go(some):
        for one in some:
            one.start()

    def arrive(some):
        for one in some:
            one.wait_recv()

    def leave(some):
        for one in some:
            one.wait_send()

    for p in range(4):
        cols_ref[p, y, x, half] = beside(c0_ref[:, 128 * p:128 * p + 128])
        go(first(p))
    for p in range(4):
        arrive(first(p))
        go(second(p))
    arrive(second(0))
    go(third(0))
    corr.summed()

    def task(t, carry):
        kp = order(t)
        k, p = kp // 4, kp % 4
        arrive(third(kp))
        leave(first(kp) + second(kp) + third(kp))

        for n in range(1, 4):
            @pl.when(p == n)
            def _():
                now = cols_ref[kp].reshape(2048, 256)
                factors = [beside(quarters(dot(q_ref[k * 4 + q], now, TN))) for q in range(n)]
                weights = [jnp.concatenate([factor, factor], axis=0) for factor in factors]
                taken = dot(q_ref[k * 4], weights[0], NN)
                for q in range(1, n):
                    taken = taken + dot(q_ref[k * 4 + q], weights[q], NN)
                cols_ref[kp] = beside(halves(now.astype(F32)) - halves(taken)).reshape(4, 4, 128, 256)

        @pl.when(t < 3)
        def _():
            arrive(second(t + 1))
            go(third(t + 1))

        now = cols_ref[kp].reshape(2048, 256)
        block = invert_block(quarters(dot(now, now, TN)))

        @pl.when((t >= 2) & (order(t - 1 + (1 - (t + 11) // 12)) < 8))
        def _():
            due = order(t - 1) + 4
            arrive(first(due))
            go(second(due))

        @pl.when(t == 2)
        def _():
            arrive(first(4))
            go(second(4))

        @pl.when((t >= 3) & (order(t - 2 + 2 * (1 - (t + 10) // 12)) < 8))
        def _():
            due = order(t - 2) + 4
            arrive(second(due))
            go(third(due))

        @pl.when(t == 3)
        def _():
            arrive(second(4))
            go(third(4))

        high, low = split(block)
        weights = jnp.concatenate(
            [jnp.concatenate([high, high], axis=1), jnp.concatenate([low, low], axis=1)], axis=0)
        for r in range(4):
            rows = pl.ds(512 * r, 512)
            q_ref[kp, rows] = beside(halves(dot(cols_ref[kp, r].reshape(512, 256), weights, NT)))

        @pl.when(t == 1)
        def _():
            corr.gathered()
            pair_ref[:64], pair_ref[64:] = split(corr.g_ref[...])
            cols_ref[4, y, x, half] = beside(quarters(dot(pair_ref[...], q_ref[0], NN)))
            go(first(4))

        @pl.when((t > 0) & (k < 2))
        def _():
            cols_ref[kp + 4, y, x, half] = beside(quarters(dot(pair_ref[...], q_ref[kp], NN)))
            go(first(kp + 4))

        @pl.when(k == 2)
        def _():
            rows = pl.ds(pl.multiple_of(head * 128, 128), 128)
            basis_ref[:, pl.ds(pl.multiple_of(p * 128, 128), 128)] = halves(q_ref[kp, rows].astype(F32))

        return carry

    lax.fori_loop(0, 12, task, 0)
    total = jnp.zeros((512, 256), F32)
    for owner in range(8):
        pair = [kv_ref[owner // 2, owner % 2 * 2 + n] for n in range(2)]
        there = q_ref[8 + head // 4, 256 * owner:256 * owner + 256]
        total = total + dot(jnp.concatenate(pair, axis=1), there, NN)
    total_ref[...] = jnp.transpose(halves(total))
    latent_ref[...] = total_ref[pl.ds(pl.multiple_of(head % 4 * 32, 32), 32), :]


def kernel(st_ref, gain_ref, w_any, bias_ref, sketch_ref, basis_ref, latent_ref, kv_ref, w_ref, sq_ref, n_ref,
           part_ref, own_ref, recv_ref, recv2_ref, whole_ref, gpart_ref, half_ref, z_ref, g_ref, cpart_ref, chalf_ref,
           cz_ref, c0_ref, cols_ref, q_ref, pair_ref, total_ref, w_sem, send_sem, recv_sem, panel_send, panel_recv):
    place = position()
    dp, head, z, c, _, _ = place
    copies = Copies(send_sem, recv_sem)

    def meet():
        greet([(dp, lax.rem(head + k, 16)) for k in range(1, 16)] + [(dp + 1 - 2 * c, head)] + [
            (lax.rem(z + k, 8) * 2 + c, head) for k in range(1, 8)])

    pending = make_kv(place, copies, st_ref, gain_ref, w_any, bias_ref, sketch_ref, kv_ref, w_ref, sq_ref, n_ref, part_ref,
            own_ref, recv_ref, recv2_ref, whole_ref, w_sem, meet)
    corr = Corr(place, copies, kv_ref, gpart_ref, half_ref, z_ref, g_ref)
    first_columns(place, copies, corr, *pending, kv_ref, whole_ref, cpart_ref, chalf_ref, cz_ref, c0_ref)
    iterate(place, corr, c0_ref, kv_ref, basis_ref, latent_ref, cols_ref, q_ref, pair_ref, total_ref, panel_send,
            panel_recv)
    copies.finish()


def finish_kernel(basis_ref, latent_ref, basis_out, latent_out):
    basis_out[...] = basis_ref[...]
    latent_out[...] = latent_ref[...]


def local(states, gain, kv_weight, kv_bias, sketch):
    n = 15 + 4 * 12 + 13 + 8 + 14 + 15
    shapes = (jax.ShapeDtypeStruct((128, 512), F32), jax.ShapeDtypeStruct((32, 512), F32))
    basis, latent = pl.pallas_call(
        kernel,
        out_shape=shapes,
        in_specs=[VM, VM, pl.BlockSpec(memory_space=pl.ANY), VM, VM],
        out_specs=(VM, VM),
        scratch_shapes=[
            pltpu.VMEM((4, 4, 512, 128), BF16),
            pltpu.VMEM((512, 2048), BF16),
            pltpu.VMEM((16, 8, 128), F32),
            pltpu.VMEM((512, 512), BF16),
            pltpu.VMEM((4, 4, 512, 128), BF16),
            pltpu.VMEM((4, 4, 128, 128), F32),
            pltpu.VMEM((4, 3, 4, 128, 128), BF16),
            pltpu.VMEM((4, 3, 128, 128), F32),
            pltpu.VMEM((4, 4, 128, 512), BF16),
            pltpu.VMEM((2, 8, 64, 256), F32),
            pltpu.VMEM((8, 64, 256), F32),
            pltpu.VMEM((7, 64, 256), F32),
            pltpu.VMEM((64, 2048), F32),
            pltpu.VMEM((2, 64, 512), F32),
            pltpu.VMEM((64, 512), F32),
            pltpu.VMEM((7, 8, 512), F32),
            pltpu.VMEM((64, 512), F32),
            pltpu.VMEM((12, 4, 4, 128, 256), BF16),
            pltpu.VMEM((12, 2048, 256), BF16),
            pltpu.VMEM((128, 2048), BF16),
            pltpu.VMEM((128, 512), F32),
            DMA,
            DMA((n,)),
            DMA((n,)),
            DMA((12, 13)),
            DMA((12, 13)),
        ],
        compiler_params=pltpu.CompilerParams(collective_id=1, has_side_effects=True, vmem_limit_bytes=60 << 20),
    )(states, gain.reshape(1, 512), kv_weight, kv_bias.reshape(1, 128), sketch)
    basis, latent = pl.pallas_call(finish_kernel, out_shape=shapes, in_specs=[VM] * 2, out_specs=(VM, VM))(basis, latent)
    return basis, latent.T


def solution(mesh):
    in_specs = (P("dp", "head"), P("head"), P("head", None), P("head"), P("head", None))
    out_specs = (P("head", None), P("dp", "head"))
    return jax.shard_map(local, mesh=mesh, in_specs=in_specs, out_specs=out_specs, check_vma=False)
```
